128 devices in a mesh: dp: 4 (over y_lo, core), basis: 32 (over z, y_hi, x).
Axes of the slice: x: 4, y: 4 (y_hi: 2, y_lo: 2; y = y_hi * 2 + y_lo), z: 4, core: 2. Of those that a mesh axis runs over, the one named last changes fastest.
Arguments:
- train_act: bfloat16 [1024, 18944], P('dp', 'basis'), may hold values from -6 to 6
- train_out_grad: bfloat16 [1024, 3584], P('dp', 'basis'), may hold values from -6 to 6
- query_act: bfloat16 [256, 18944], P('dp', 'basis'), may hold values from -6 to 6
- query_out_grad: bfloat16 [256, 3584], P('dp', 'basis'), may hold values from -6 to 6
- in_basis: bfloat16 [18944, 18944], P('dp', 'basis'), may hold values from -0.046875 to 0.046875
- out_basis: bfloat16 [3584, 3584], P('basis'), may hold values from -0.09375 to 0.09375
- eigvals: bfloat16 [3584, 18944], P(None, 'basis'), may hold values from 0.5 to 8
- pair_ids: int32 [256], replicated, may hold values from 0 to 3
- seq_lengths: int32 [4, 4], P('dp'), may hold values from 1 to 128, 256 in all within a row
Outputs:
- scores: float32 [4, 16], P(None, 'dp')
The draws below stay inside these ranges and needn't reach their ends.
Inputs may be any that keep to these rules, and one draw needn't show every extreme that they name: `seq_lengths`: each row sums to 256, and its largest entry is 128.
All inputs are finite; a program needn't handle non-finite values.
Results may differ from the reference program's by a relative error of at most 0.0075.
Values may be sent and summed in bfloat16 or wider, within the bound.
A program may use at most 192 MiB of HBM per device.

```python
import math
import jax
import jax.numpy as jnp
import numpy as np
from jax import lax

D = 3584
FF = 18944
PAIRS = 4
SEQ_DP = 4
TOK_DP = 256
QTOK_DP = 64
MOST_LEN = 128
TOKENS = 1024
QTOKENS = 256
SEQS = 16
N_DP = 4


def set_ends(values, key, low, high):
    shape = values.shape
    index_at = [jax.random.randint(jax.random.fold_in(key, axis), (), 0, shape[axis]) for axis in range(len(shape))]
    values = values.at[tuple(index_at)].set(low)
    longest = shape.index(max(shape))
    index_at[longest] = (index_at[longest] + 1) % shape[longest]
    return values.at[tuple(index_at)].set(high)


def steps_of(stream_key, extent, pieces, low, largest):
    gain = 1.0
    for dim, shards_of in pieces:
        draws = jax.random.uniform(jax.random.fold_in(jax.random.fold_in(stream_key, 6), dim), (shards_of,), jnp.float32, low / len(pieces), largest / len(pieces))
        gain = gain * jnp.repeat(jnp.exp(draws), extent[dim] // shards_of).reshape((-1,) + (1,) * (len(extent) - 1 - dim))
    return gain


def split_up(count, total, bound, lean):
    weights = [(1 << 20) // math.isqrt(grade ** lean) + 1 for grade in range(2, count + 1)]
    rest, holding = total - bound - (count - 1), [1] * (count - 1)
    while rest > 0:
        candidates = [i for i in range(count - 1) if holding[i] < bound]
        whole, budget = sum([weights[i] for i in candidates]), rest
        for i in candidates:
            addition = min(bound - holding[i], max(1, budget * weights[i] // whole), rest)
            holding[i] = holding[i] + addition
            rest = rest - addition
    return np.array([bound] + holding)


def ragged_sizes(stream_key, amount, total, reach, lean):
    if amount == 2:
        one = jax.random.randint(stream_key, (), max(1, total - reach), min(reach, total - 1) + 1)
        return jnp.stack([one, total - one])
    tallies = jnp.asarray(split_up(amount, total, reach, lean), jnp.int32)
    pairs = (amount - 1) // 2
    giver, sink = tallies[1:1 + 2 * pairs:2], tallies[2:2 + 2 * pairs:2]
    slack = jnp.minimum(giver - 1, reach - sink)
    passed = jax.random.randint(jax.random.fold_in(stream_key, 1), (pairs,), 0, 1 << 20) % (slack + 1)
    tallies = tallies.at[1:1 + 2 * pairs:2].set(giver - passed).at[2:2 + 2 * pairs:2].set(sink + passed)
    return tallies[jax.random.permutation(jax.random.fold_in(stream_key, 2), amount)]


def scatter_about(stream_key, shape, deviation, limit, pieces=(), kind=jnp.bfloat16):
    result = deviation * jax.random.normal(stream_key, shape, jnp.float32)
    if pieces:
        result = result * steps_of(stream_key, shape, pieces, -0.22, 0.18)
    return jnp.clip(result, -limit, limit).astype(kind)


def setup_inputs(seed: int = 0) -> dict:
    key_list = jax.random.split(jax.random.key(seed), 10)
    train_act = scatter_about(key_list[0], (TOKENS, FF), 1.0, 6.0, ((0, 4), (1, 32)))
    train_out_grad = scatter_about(key_list[1], (TOKENS, D), 1.0, 6.0, ((0, 4), (1, 32)))
    query_act = scatter_about(key_list[2], (QTOKENS, FF), 1.0, 6.0, ((0, 4), (1, 32)))
    query_out_grad = scatter_about(key_list[3], (QTOKENS, D), 1.0, 6.0, ((0, 4), (1, 32)))
    in_basis = scatter_about(key_list[4], (FF, FF), FF ** -0.5, 0.046875, ((0, 4), (1, 32)))
    out_basis = scatter_about(key_list[5], (D, D), D ** -0.5, 0.09375, ((0, 32),))
    eigvals = jnp.clip(jnp.exp(math.log(8.0) - 2.7725887 * jax.random.uniform(key_list[6], (D, FF), jnp.float32) ** steps_of(key_list[6], (D, FF), ((1, 32),), -0.2, 0.2)), 0.5, 8.0).astype(jnp.bfloat16)
    pair_ids = set_ends(jax.random.randint(key_list[7], (QTOKENS,), 0, PAIRS), jax.random.fold_in(key_list[7], 1), 0, PAIRS - 1).astype(jnp.int32)
    seq_lengths = jax.vmap(lambda own: ragged_sizes(own, SEQ_DP, TOK_DP, MOST_LEN, 2))(jax.random.split(key_list[8], N_DP)).reshape((N_DP, SEQ_DP)).astype(jnp.int32)
    return dict(train_act=train_act, train_out_grad=train_out_grad, query_act=query_act, query_out_grad=query_out_grad, in_basis=in_basis, out_basis=out_basis, eigvals=eigvals, pair_ids=pair_ids, seq_lengths=seq_lengths)


DAMPING = 0.5

def reference(train_act, train_out_grad, query_act, query_out_grad, in_basis, out_basis, eigvals, pair_ids, seq_lengths):
    rot_train = jnp.dot(train_act, in_basis, preferred_element_type=jnp.float32).astype(jnp.bfloat16)
    rot_query = jnp.dot(query_act, in_basis, preferred_element_type=jnp.float32).astype(jnp.bfloat16)
    grad_train = jnp.dot(train_out_grad, out_basis, preferred_element_type=jnp.float32).astype(jnp.bfloat16)
    grad_query = jnp.dot(query_out_grad, out_basis, preferred_element_type=jnp.float32).astype(jnp.bfloat16)
    hot_table = (pair_ids[None, :] == jnp.arange(PAIRS, dtype=jnp.int32)[:, None]).astype(jnp.bfloat16)
    seq_ends = jnp.cumsum(seq_lengths, axis=1)
    seq_starts = seq_ends - seq_lengths
    positions = jnp.arange(TOK_DP, dtype=jnp.int32)
    member = ((positions[None, None, :] >= seq_starts[:, :, None]) & (positions[None, None, :] < seq_ends[:, :, None])).astype(jnp.float32)
    grad_wide = grad_train.astype(jnp.float32)
    divisor = eigvals.astype(jnp.float32) + DAMPING

    def one_pair(hot_row):
        masked = grad_query * hot_row[:, None]
        query_rot = jnp.dot(masked.T, rot_query, preferred_element_type=jnp.float32)
        precond = (query_rot / divisor).astype(jnp.bfloat16)
        projected = jnp.dot(rot_train, precond.T, preferred_element_type=jnp.float32)
        token_score = lax.optimization_barrier(jnp.sum(projected * grad_wide, axis=1))
        grouped = token_score.reshape(N_DP, TOK_DP)
        return lax.optimization_barrier(jnp.sum(member * grouped[:, None, :], axis=2)).reshape(SEQS)
    score_scale = SEQ_DP / math.sqrt(D * FF * TOK_DP * QTOK_DP)
    return lax.map(one_pair, hot_table) * score_scale
```

```python
import functools
import math

import jax
import jax.numpy as jnp
from jax import lax
from jax.experimental import pallas as pl
from jax.experimental.pallas import tpu as pltpu
from jax.sharding import PartitionSpec as P

D = 3584
FF = 18944
PAIRS = 4
SEQ_DP = 4
TOK_DP = 256
QTOK_DP = 64
ROWS = TOK_DP + QTOK_DP
COLS = FF // 32

DAMPING = 0.5
MESH = pl.DeviceIdType.MESH

UNIT = 2 * ROWS
RB = 384


def place():
    dp, b = lax.axis_index("dp"), lax.axis_index("basis")
    x, y, z, c = b % 4, ((b // 4) % 2) * 2 + dp // 2, b // 8, dp % 2
    return x, y, z, c


def device(x, y, z, c):
    x, y, z = (x + 4) % 4, (y + 4) % 4, (z + 4) % 4
    return ((y % 2) * 2 + c, z * 8 + (y // 2) * 4 + x)


def turn(i):
    return jnp.where(i == 2, 3, jnp.where(i == 3, 2, i))


def rotate_kernel(act, w_hbm, out, units, other, w, w_sem, own_sem, s0, r0, rb, ra, rob, roa, szb, syb, sxb, sxa, sya, sya2, sza):
    x, y, z, c = place()
    d = 2 * (y % 2) + c
    zeta = (z - d + 4) % 4
    sign = 1 - 2 * c
    pi = (sign * zeta + 4) % 4
    is_own, is_other = zeta == 0, zeta == 2

    def slot(xs, ys):
        return ((xs + 4) % 4) * 4 + (ys + 4) % 4

    here = slot(x, y)
    beta, alpha = pl.ds(0, RB), pl.ds(RB, UNIT - RB)

    def copy(src, dst, send, recv, target):
        return pltpu.make_async_remote_copy(
            src_ref=src, dst_ref=dst, send_sem=send, recv_sem=recv, device_id=target, device_id_type=MESH
        )

    partners = [device(x + o, y, z, c) for o in (1, 2, 3)]
    partners += [device(x, y + o, z, c) for o in (1, 2, 3)]
    partners += [device(x, y, z + o, c) for o in (1, 2, 3)]
    partners += [device(x, y, z, 1 - c)]
    core = partners[-1]

    w_copy = pltpu.make_async_copy(w_hbm, w, w_sem)
    w_copy.start()
    barrier = pltpu.get_barrier_semaphore()
    for p in partners:
        pl.semaphore_signal(barrier, inc=1, device_id=p, device_id_type=MESH)
    pl.semaphore_wait(barrier, len(partners))

    mine = pl.ds(pl.multiple_of(c * ROWS, ROWS), ROWS)
    theirs = pl.ds(pl.multiple_of((1 - c) * ROWS, ROWS), ROWS)
    partner_zeta = (zeta - sign + 4) % 4
    to_units = copy(act, units.at[here, mine], s0, r0, core)
    to_other = copy(act, other.at[x, mine], s0, r0, core)

    @pl.when(partner_zeta == 0)
    def _():
        to_units.start()

    @pl.when(partner_zeta == 2)
    def _():
        to_other.start()

    own_units = pltpu.make_async_copy(act, units.at[here, mine], own_sem)
    own_other = pltpu.make_async_copy(act, other.at[x, mine], own_sem)

    @pl.when(is_own)
    def _():
        own_units.start()
        own_units.wait()
        copy(act, units.at[here, theirs], s0, r0, core).wait_recv()

    @pl.when(is_other)
    def _():
        own_other.start()
        own_other.wait()
        copy(act, other.at[x, theirs], s0, r0, core).wait_recv()

    def z_beta(i, from_units):
        target = device(x, y, z + (1, 3, 2)[i], c)
        if from_units:
            piece = units.at[here, beta]
            return copy(piece, piece, szb.at[i], rb.at[here], target)
        piece = other.at[x, beta]
        return copy(piece, piece, szb.at[i], rob, target)

    def x_alpha(i, from_units):
        target = device(x + (1, 3, 2)[i], y, z, c)
        if from_units:
            piece = units.at[here, alpha]
            return copy(piece, piece, sxa.at[i], ra.at[here], target)
        piece = other.at[x, alpha]
        return copy(piece, piece, sxa.at[i], roa.at[x], target)

    def z_alpha(t, s):
        piece = units.at[s, alpha]
        return copy(piece, piece, sza.at[t], ra.at[s], device(x, y, z + sign, c))

    def y_alpha_own(t, s):
        piece = units.at[s, alpha]
        return copy(piece, piece, sya.at[t], ra.at[s], device(x, y + 2, z, c))

    def y_alpha_other(t, xs, step):
        s = slot(xs, y)
        sems = sya if step == 1 else sya2
        return copy(other.at[xs, alpha], units.at[s, alpha], sems.at[t], ra.at[s], device(x, y + step, z, c))

    def y_beta_own():
        piece = units.at[here, beta]
        return copy(piece, piece, syb.at[2], rb.at[here], device(x, y + 2, z, c))

    def y_beta_other(i):
        return copy(other.at[x, beta], units.at[here, beta], syb.at[i], rb.at[here], device(x, y + (1, 3)[i], z, c))

    def x_beta(n, s, step):
        piece = units.at[s, beta]
        return copy(piece, piece, sxb.at[n], rb.at[s], device(x + step, y, z, c))

    @pl.when(is_own)
    def _():
        for i in range(3):
            z_beta(i, True).start()
            x_alpha(i, True).start()

    @pl.when(is_other)
    def _():
        for i in range(3):
            z_beta(i, False).start()
            x_alpha(i, False).start()

    out[...] = jnp.zeros_like(out)
    w_copy.wait()

    def step(t, carry):
        a_x, a_y = (x + turn(t % 4)) % 4, (y + turn(t // 4)) % 4
        b_x, b_y = (x + turn(t // 4)) % 4, (y + turn(t % 4)) % 4
        a_slot, b_slot = slot(a_x, a_y), slot(b_x, b_y)
        first = t < 4

        @pl.when(first & is_other)
        def _():
            @pl.when(t > 0)
            def _():
                copy(other.at[a_x, alpha], other.at[a_x, alpha], s0, roa.at[a_x], core).wait_recv()

            y_alpha_other(t, a_x, 1).start()
            y_alpha_other(t, a_x, 3).start()

        @pl.when(t == 0)
        def _():
            @pl.when(jnp.logical_not(is_other))
            def _():
                copy(other.at[x, beta], other.at[x, beta], s0, rob, core).wait_recv()

            y_beta_other(0).start()
            y_beta_other(1).start()

        @pl.when(jnp.logical_not(is_own & (t == 0)))
        def _():
            copy(units.at[b_slot, beta], units.at[b_slot, beta], s0, rb.at[b_slot], core).wait_recv()

        @pl.when(t == 0)
        def _():
            y_beta_own().start()

        @pl.when(first)
        def _():
            x_beta(2 * t, b_slot, 1).start()
            x_beta(2 * t + 1, b_slot, 3).start()

        @pl.when((t == 6) | (t == 7))
        def _():
            x_beta(t + 2, b_slot, 3).start()

        @pl.when((t == 8) | (t == 9))
        def _():
            x_beta(t + 2, b_slot, 1).start()

        @pl.when(jnp.logical_not(is_own & (t == 0)))
        def _():
            copy(units.at[a_slot, alpha], units.at[a_slot, alpha], s0, ra.at[a_slot], core).wait_recv()

        @pl.when(pi != 3)
        def _():
            z_alpha(t, a_slot).start()

        @pl.when(is_own & first)
        def _():
            y_alpha_own(t, a_slot).start()

        out[b_y % 2, beta, :] += jnp.dot(
            units[b_slot, beta, :], w[4 * (b_y // 2) + b_x], preferred_element_type=jnp.float32
        )
        out[a_y % 2, alpha, :] += jnp.dot(
            units[a_slot, alpha, :], w[4 * (a_y // 2) + a_x], preferred_element_type=jnp.float32
        )
        return carry

    lax.fori_loop(0, 16, step, 0)

    @pl.when(partner_zeta == 0)
    def _():
        to_units.wait_send()

    @pl.when(partner_zeta == 2)
    def _():
        to_other.wait_send()

    for i in range(2):
        y_beta_other(i).wait_send()
    y_beta_own().wait_send()

    @pl.when(is_own | is_other)
    def _():
        for i in range(3):
            z_beta(i, True).wait_send()
            x_alpha(i, True).wait_send()

    def drain_first(t, carry):
        @pl.when(is_own | is_other)
        def _():
            y_alpha_own(t, here).wait_send()

        @pl.when(is_other)
        def _():
            y_alpha_other(t, x, 3).wait_send()

        return carry

    lax.fori_loop(0, 4, drain_first, 0)

    def drain_x(t, carry):
        x_beta(t, here, 1).wait_send()
        return carry

    lax.fori_loop(0, 12, drain_x, 0)

    @pl.when(pi != 3)
    def _():
        def drain_z(t, carry):
            z_alpha(t, here).wait_send()
            return carry

        lax.fori_loop(0, 16, drain_z, 0)


def rotate(act_rows, in_basis):
    dma = pltpu.SemaphoreType.DMA
    return pl.pallas_call(
        rotate_kernel,
        out_shape=jax.ShapeDtypeStruct((2, UNIT, COLS), jnp.float32),
        in_specs=[pl.BlockSpec(memory_space=pltpu.VMEM), pl.BlockSpec(memory_space=pl.ANY)],
        out_specs=pl.BlockSpec(memory_space=pltpu.VMEM),
        scratch_shapes=[
            pltpu.VMEM((16, UNIT, COLS), jnp.bfloat16),
            pltpu.VMEM((4, UNIT, COLS), jnp.bfloat16),
            pltpu.VMEM((8, COLS, COLS), jnp.bfloat16),
            dma,
            dma,
            dma,
            dma,
            dma((16,)),
            dma((16,)),
            dma,
            dma((4,)),
            dma((3,)),
            dma((3,)),
            dma((12,)),
            dma((3,)),
            dma((4,)),
            dma((4,)),
            dma((16,)),
        ],
        compiler_params=pltpu.CompilerParams(
            collective_id=0, has_side_effects=True, vmem_limit_bytes=56 * 2**20
        ),
        cost_estimate=pl.CostEstimate(flops=2 * 1280 * 4736 * 592, bytes_accessed=20 * 2**20, transcendentals=0),
        name="rotate",
    )(act_rows, in_basis.reshape(8, COLS, COLS))


def on_device(
    train_act,
    train_out_grad,
    query_act,
    query_out_grad,
    in_basis,
    out_basis,
    eigvals,
    pair_ids,
    seq_lengths,
):
    tok_rows = train_act.shape[0]
    act_rows = jnp.concatenate([train_act, query_act], axis=0)
    grad_rows = jnp.concatenate([train_out_grad, query_out_grad], axis=0)
    partial = rotate(act_rows, in_basis)
    rotated = lax.psum(partial, "dp").astype(jnp.bfloat16).reshape(4, ROWS, COLS)
    contract = (((0,), (1,)), ((), ()))
    grad_term = lax.dot_general(out_basis, grad_rows, contract, preferred_element_type=jnp.float32)
    rot_grad = lax.psum(grad_term, "basis").astype(jnp.bfloat16)
    query_rot_act = rotated[:, tok_rows:].reshape(4 * QTOK_DP, COLS)
    train_rot_act = lax.dynamic_index_in_dim(rotated, lax.axis_index("dp"), keepdims=False)[:tok_rows]
    query_rot_grad = lax.all_gather(rot_grad[:, tok_rows:], "dp", axis=1, tiled=True)
    hot_table = (pair_ids[None, :] == jnp.arange(PAIRS, dtype=jnp.int32)[:, None]).astype(
        jnp.bfloat16
    )
    masked = query_rot_grad[None, :, :] * hot_table[:, None, :]
    query_rot = jnp.einsum("pdq,qj->pdj", masked, query_rot_act, preferred_element_type=jnp.float32)
    precond = (query_rot / (eigvals.astype(jnp.float32) + DAMPING)).astype(jnp.bfloat16)
    projected = jnp.einsum(
        "pdj,tj->pdt", precond, train_rot_act, preferred_element_type=jnp.float32
    )
    token_score = jnp.sum(
        projected * rot_grad[:, :tok_rows].astype(jnp.float32)[None, :, :], axis=1
    )
    lengths = seq_lengths[0]
    seq_ends = jnp.cumsum(lengths)
    seq_starts = seq_ends - lengths
    positions = jnp.arange(tok_rows, dtype=jnp.int32)
    member = (
        (positions[None, :] >= seq_starts[:, None]) & (positions[None, :] < seq_ends[:, None])
    ).astype(jnp.float32)
    partial_scores = jnp.dot(token_score, member.T, preferred_element_type=jnp.float32)
    score_scale = SEQ_DP / math.sqrt(D * FF * TOK_DP * QTOK_DP)
    return lax.psum(partial_scores, "basis") * score_scale


def solution(mesh):
    in_specs = (
        P("dp", "basis"),
        P("dp", "basis"),
        P("dp", "basis"),
        P("dp", "basis"),
        P("dp", "basis"),
        P("basis", None),
        P(None, "basis"),
        P(),
        P("dp", None),
    )
    out_specs = P(None, "dp")
    return jax.shard_map(
        on_device, mesh=mesh, in_specs=in_specs, out_specs=out_specs, check_vma=False
    )
```

```python
import functools
import math

import jax
import jax.numpy as jnp
from jax import lax
from jax.experimental import pallas as pl
from jax.experimental.pallas import tpu as pltpu
from jax.sharding import PartitionSpec as P

D = 3584
FF = 18944
PAIRS = 4
SEQ_DP = 4
TOK_DP = 256
QTOK_DP = 64
ROWS = TOK_DP + QTOK_DP
COLS = FF // 32
DEPTH = FF // 4
FEAT = D // 32
QUART = D // 4
LANES = 2 * ROWS
TRAIN = 2 * TOK_DP
CHUNK = ROWS // 4

DAMPING = 0.5
SCALE = SEQ_DP / math.sqrt(D * FF * TOK_DP * QTOK_DP)
MESH = pl.DeviceIdType.MESH
F32, BF16 = jnp.float32, jnp.bfloat16

RB = 336
OTHER = (1, 3, 2)


def place():
    dp, b = lax.axis_index("dp"), lax.axis_index("basis")
    return b % 4, ((b // 4) % 2) * 2 + dp // 2, b // 8, dp % 2


def device(x, y, z, c):
    x, y, z = (x + 4) % 4, (y + 4) % 4, (z + 4) % 4
    return ((y % 2) * 2 + c, z * 8 + (y // 2) * 4 + x)


class Sems:
    def __init__(self):
        self.used = 0

    def take(self, n=1):
        self.used += n
        return self.used - n


N_SEMS = 200


def kernel(
    train_t, query, train_g_t, query_g, pid, lengths, w_hbm, eig_hbm, ob_hbm, out,
    units, other, w, acc, query_t, query_in, eig, recip,
    og_tok, og_feat, ob, g_sum, g_part, g_rz, g_yb, g_ry, g_full, g_train_t,
    sum_in, chip_out, chip_in, rot, precond, tok, tok_in, tok_y, tok_yin, red_x, red_z, red_y,
    sems,
):
    x, y, z, c = place()
    k = y % 2
    d = 2 * k + c
    zeta = (z - d + 4) % 4
    sign = 1 - 2 * c
    pi = (sign * zeta + 4) % 4
    is_own, is_other = zeta == 0, zeta == 2
    names = Sems()

    def sem(base, i=0):
        return sems.at[base + i]

    def slot(xs, ys):
        return ((xs + 4) % 4) * 4 + (ys + 4) % 4

    def unit(xs, ys, low, count, lanes=None):
        xs, ys = (xs + 4) % 4, (ys + 4) % 4
        rows = pl.ds(pl.multiple_of(COLS * (4 * (ys // 2) + xs) + low, 16), count)
        return units.at[ys % 2, rows] if lanes is None else units.at[ys % 2, rows, lanes]

    def beta(xs, ys):
        return unit(xs, ys, 0, RB)

    def alpha(xs, ys):
        return unit(xs, ys, RB, COLS - RB)

    def copy(src, dst, send, recv, target):
        return pltpu.make_async_remote_copy(
            src_ref=src, dst_ref=dst, send_sem=send, recv_sem=recv, device_id=target, device_id_type=MESH
        )

    partners = [device(x + o, y, z, c) for o in OTHER]
    partners += [device(x, y + o, z, c) for o in OTHER]
    partners += [device(x, y, z + o, c) for o in OTHER]
    core = device(x, y, z, 1 - c)
    partners += [core]
    mate = device(x, y + 1 - 2 * k, z, c)

    def landed(dst, recv):
        copy(dst, dst, sem(dummy), recv, core).wait_recv()

    sent = []

    def send(src, dst, s, r, target):
        cp = copy(src, dst, s, r, target)
        cp.start()
        sent.append(cp)

    dummy = names.take()
    s_w, s_eig, s_ob, s_own = names.take(), names.take(), names.take(), names.take()
    s_step, r_step = names.take(2), names.take(2)
    r_b, r_a, r_ob, r_oa = names.take(16), names.take(16), names.take(), names.take(4)
    s_zb, s_yb, s_xb = names.take(3), names.take(3), names.take(12)
    s_xa, s_ya, s_ya2, s_za = names.take(3), names.take(4), names.take(4), names.take(16)

    w_copy = pltpu.make_async_copy(w_hbm, w, sem(s_w))
    w_copy.start()
    quarter = pl.ds(pl.multiple_of(d * QUART, 128), QUART)
    ob_copy = pltpu.make_async_copy(ob_hbm.at[:, quarter], ob.at[x], sem(s_ob))
    ob_copy.start()
    eig_copy = pltpu.make_async_copy(eig_hbm.at[:, quarter], eig, sem(s_eig))
    eig_copy.start()

    barrier = pltpu.get_barrier_semaphore()
    for p in partners:
        pl.semaphore_signal(barrier, inc=1, device_id=p, device_id_type=MESH)
    pl.semaphore_wait(barrier, len(partners))

    turned = query[...].astype(F32).T.astype(BF16)
    nothing = jnp.zeros_like(turned)
    query_t[...] = jnp.concatenate(
        [jnp.where(c == 0, turned, nothing), jnp.where(c == 1, turned, nothing)], axis=1
    )
    og_tok[d, 0:TOK_DP, :] = train_g_t[...].astype(F32).T.astype(BF16)
    og_tok[d, TOK_DP:, :] = query_g[...]

    gs_c, gr_c = names.take(), names.take()
    send(og_tok.at[d], og_tok.at[d], sem(gs_c), sem(gr_c), core)

    mine = pl.ds(pl.multiple_of(c * TOK_DP, 128), TOK_DP)
    theirs = pl.ds(pl.multiple_of((1 - c) * TOK_DP, 128), TOK_DP)
    tail = pl.ds(TRAIN, LANES - TRAIN)
    partner_zeta = (zeta - sign + 4) % 4
    to_units = copy(train_t, unit(x, y, 0, COLS, mine), sem(s_step), sem(r_step), core)
    to_other = copy(train_t, other.at[x, :, mine], sem(s_step), sem(r_step), core)
    to_query = copy(query_t, query_in, sem(s_step, 1), sem(r_step, 1), core)

    @pl.when(partner_zeta == 0)
    def _():
        to_units.start()

    @pl.when(partner_zeta == 2)
    def _():
        to_other.start()

    @pl.when((partner_zeta == 0) | (partner_zeta == 2))
    def _():
        to_query.start()

    def z_beta(i, own):
        piece = beta(x, y) if own else other.at[x, pl.ds(0, RB)]
        return copy(piece, piece, sem(s_zb, i), sem(r_b, slot(x, y)) if own else sem(r_ob), device(x, y, z + OTHER[i], c))

    def x_alpha(i, own):
        piece = alpha(x, y) if own else other.at[x, pl.ds(RB, COLS - RB)]
        return copy(piece, piece, sem(s_xa, i), sem(r_a, slot(x, y)) if own else sem(r_oa, x), device(x + OTHER[i], y, z, c))

    def z_alpha(t, xs, ys):
        piece = alpha(xs, ys)
        return copy(piece, piece, sem(s_za, t), sem(r_a, slot(xs, ys)), device(x, y, z + sign, c))

    def y_alpha_own(i, xs):
        piece = alpha(xs, y)
        return copy(piece, piece, sem(s_ya, i), sem(r_a, slot(xs, y)), device(x, y + 2, z, c))

    def y_alpha_other(i, xs, step):
        src = other.at[xs, pl.ds(RB, COLS - RB)]
        return copy(src, alpha(xs, y), sem(s_ya if step == 1 else s_ya2, i), sem(r_a, slot(xs, y)), device(x, y + step, z, c))

    def y_beta_own():
        piece = beta(x, y)
        return copy(piece, piece, sem(s_yb, 2), sem(r_b, slot(x, y)), device(x, y + 2, z, c))

    def y_beta_other(i):
        src = other.at[x, pl.ds(0, RB)]
        return copy(src, beta(x, y), sem(s_yb, i), sem(r_b, slot(x, y)), device(x, y + OTHER[i], z, c))

    def x_beta(n, xs, ys, step):
        piece = beta(xs, ys)
        return copy(piece, piece, sem(s_xb, n), sem(r_b, slot(xs, ys)), device(x + step, y, z, c))

    def gather_step(dst_mine, dst_theirs, dst_tail):
        own = pltpu.make_async_copy(train_t, dst_mine, sem(s_own))
        own.start()
        own.wait()
        landed(query_in, sem(r_step, 1))
        dst_tail[...] = query_t[...] + query_in[...]
        landed(dst_theirs, sem(r_step))

    @pl.when(is_own)
    def _():
        gather_step(unit(x, y, 0, COLS, mine), unit(x, y, 0, COLS, theirs), unit(x, y, 0, COLS, tail))
        for i in range(3):
            z_beta(i, True).start()
            x_alpha(i, True).start()

    @pl.when(is_other)
    def _():
        gather_step(other.at[x, :, mine], other.at[x, :, theirs], other.at[x, :, tail])
        for i in range(3):
            z_beta(i, False).start()
            x_alpha(i, False).start()
        y_alpha_other(0, x, 1).start()
        y_alpha_other(0, x, 3).start()

    @pl.when(is_own)
    def _():
        y_alpha_own(0, x).start()

    gs_y, gr_y = names.take(2), names.take(2)
    landed(og_tok.at[2 * k + 1 - c], sem(gr_c))
    send(og_tok.at[2 * k], og_tok.at[2 * k], sem(gs_y), sem(gr_y), mate)
    send(og_tok.at[2 * k + 1], og_tok.at[2 * k + 1], sem(gs_y, 1), sem(gr_y, 1), mate)
    ob_copy.wait()
    gs_ob, gr_ob = names.take(3), names.take(4)
    for i, o in enumerate(OTHER):
        send(ob.at[x], ob.at[x], sem(gs_ob, i), sem(gr_ob, x), device(x + o, y, z, c))

    ALPHA = [(0, 0), (1, 0), (3, 0), (2, 0), (0, 2), (0, 1), (0, 3), (1, 2), (3, 2), (2, 2)]
    ALPHA += [(1, 1), (1, 3), (3, 1), (3, 3), (2, 1), (2, 3)]
    BETA = (0, 2, 1, 3)

    def on_x(o):
        return (x + o) % 4

    def on_y(o):
        return (y + o) % 4

    def alphas(first, last):
        for t in range(first, last):
            dx, dy = ALPHA[t]
            xs, ys = on_x(dx), on_y(dy)
            if (dx, dy) == (0, 0):

                @pl.when(jnp.logical_not(is_own))
                def _():
                    landed(alpha(xs, ys), sem(r_a, slot(xs, ys)))
            else:
                landed(alpha(xs, ys), sem(r_a, slot(xs, ys)))

            @pl.when(pi != 3)
            def _():
                z_alpha(t, xs, ys).start()

    def own_beta(i):
        ys = on_y(BETA[i])
        if i == 0:

            @pl.when(jnp.logical_not(is_own))
            def _():
                landed(beta(x, ys), sem(r_b, slot(x, ys)))
        else:
            landed(beta(x, ys), sem(r_b, slot(x, ys)))
        x_beta(2 * i, x, ys, 1).start()
        x_beta(2 * i + 1, x, ys, 3).start()

    def side_beta(i):
        ys = on_y(BETA[i])
        order = ((3, 1), (1, 3))[i % 2]
        for n, dx in enumerate(order):
            landed(beta(on_x(dx), ys), sem(r_b, slot(on_x(dx), ys)))
            if n == 0:
                x_beta(8 + i, on_x(dx), ys, 4 - dx).start()

    def far_beta(i):
        ys = on_y(BETA[i])
        landed(beta(on_x(2), ys), sem(r_b, slot(on_x(2), ys)))

    own_beta(0)
    y_beta_own().start()

    @pl.when(jnp.logical_not(is_other))
    def _():
        landed(other.at[x, pl.ds(0, RB)], sem(r_ob))

    y_beta_other(0).start()
    y_beta_other(1).start()
    alphas(0, 2)

    landed(og_tok.at[2 * (1 - k)], sem(gr_y))
    landed(og_tok.at[2 * (1 - k) + 1], sem(gr_y, 1))
    gs_f, gr_f = names.take(3), names.take(4)
    for i, o in enumerate(OTHER):
        q = (x + o) % 4
        send(og_tok.at[q], og_feat.at[x], sem(gs_f, i), sem(gr_f, x), device(x + o, y, z, c))
    og_feat[x] = og_tok[x]

    own_beta(1)
    alphas(2, 4)

    @pl.when(is_own)
    def _():
        for i, dx in enumerate(OTHER):
            y_alpha_own(i + 1, on_x(dx)).start()

    @pl.when(is_other)
    def _():
        for i, dx in enumerate(OTHER):
            landed(other.at[on_x(dx), pl.ds(RB, COLS - RB)], sem(r_oa, on_x(dx)))
            y_alpha_other(i + 1, on_x(dx), 1).start()
            y_alpha_other(i + 1, on_x(dx), 3).start()

    side_beta(0)
    for o in OTHER:
        xs = (x + o) % 4
        landed(og_feat.at[xs], sem(gr_f, xs))
        landed(ob.at[xs], sem(gr_ob, xs))

    def feature_block(i, carry):
        g_sum[...] += jnp.dot(og_feat[i], ob[i], preferred_element_type=F32)
        return carry

    g_sum[...] = jnp.zeros_like(g_sum)
    lax.fori_loop(0, 4, feature_block, 0)
    g_part[...] = g_sum[...].astype(BF16)

    def chunk(zz):
        return pl.ds(pl.multiple_of(((zz + 4) % 4) * CHUNK, 16), CHUNK)

    gs_z, gr_z = names.take(3), names.take(4)
    for i, o in enumerate(OTHER):
        send(g_part.at[chunk(z + o)], g_rz.at[z], sem(gs_z, i), sem(gr_z, z), device(x, y, z + o, c))

    eig_copy.wait()
    recip[...] = 1.0 / (eig[...].astype(F32) + DAMPING)

    own_beta(2)
    own_beta(3)
    alphas(4, 5)
    side_beta(1)
    alphas(5, 6)
    total = g_sum[chunk(z), :]
    for o in OTHER:
        zz = (z + o) % 4
        landed(g_rz.at[zz], sem(gr_z, zz))
        total = total + g_rz[zz].astype(F32)
    g_sum[chunk(z), :] = total
    g_yb[...] = total.astype(BF16)
    gs_h, gr_h = names.take(), names.take()
    send(g_yb, g_ry, sem(gs_h), sem(gr_h), device(x, y + 2, z, c))

    alphas(6, 8)
    landed(g_ry, sem(gr_h))
    g_full[x, chunk(z), :] = (g_sum[chunk(z), :] + g_ry[...].astype(F32)).astype(BF16)
    gs_g, gr_g = names.take(3), names.take(4)
    for i, o in enumerate(OTHER):
        piece = g_full.at[x, chunk(z)]
        send(piece, piece, sem(gs_g, i), sem(gr_g, z), device(x, y, z + o, c))

    side_beta(2)
    alphas(8, 9)
    for o in OTHER:
        zz = (z + o) % 4
        landed(g_full.at[x, chunk(zz)], sem(gr_g, zz))
    gs_x, gr_x = names.take(4), names.take(4)
    half_a, half_b = pl.ds(0, ROWS // 2), pl.ds(ROWS // 2, ROWS // 2)
    right, left = device(x + 1, y, z, c), device(x + 3, y, z, c)
    send(g_full.at[x], g_full.at[x], sem(gs_x), sem(gr_x), right)
    send(g_full.at[x], g_full.at[x], sem(gs_x, 1), sem(gr_x, 1), left)

    alphas(9, 10)
    far_beta(0)
    far_beta(1)
    x_prev, x_next, x_far = (x + 3) % 4, (x + 1) % 4, (x + 2) % 4
    w_copy.wait()

    def product(yl):
        acc[yl] = jnp.dot(w[:, 4608:], units[yl, 4608:, :], preferred_element_type=F32)

        def body(i, carry):
            rows = pl.ds(pl.multiple_of(i * 768, 128), 768)
            acc[yl] += jnp.dot(w[:, rows], units[yl, rows, :], preferred_element_type=F32)
            return carry

        lax.fori_loop(0, 6, body, 0)

    s_c1, r_c1, s_m, r_m, s_c2, r_c2 = (names.take() for _ in range(6))

    early, late = k, 1 - k
    sums_early = c == early

    def to_core(yl):
        return copy(acc.at[yl], sum_in, sem(s_c1), sem(r_c1), core)

    def to_mate():
        return copy(chip_out, chip_in, sem(s_m), sem(r_m), mate)

    def back_to_core(yl):
        return copy(rot.at[yl], rot.at[yl], sem(s_c2), sem(r_c2), core)

    def chip_sum(yl):
        landed(sum_in, sem(r_c1))
        acc[yl] += sum_in[...]
        chip_out[...] = acc[yl].astype(BF16)
        to_mate().start()

    def finish(yl):
        landed(chip_in, sem(r_m))
        rot[yl] = (acc[yl] + chip_in[...].astype(F32)).astype(BF16)
        back_to_core(yl).start()

    product(early)

    @pl.when(jnp.logical_not(sums_early))
    def _():
        to_core(early).start()

    alphas(10, 12)
    side_beta(3)
    landed(g_full.at[x_prev], sem(gr_x))
    send(g_full.at[x_prev, half_a], g_full.at[x_prev, half_a], sem(gs_x, 2), sem(gr_x, 2), right)
    landed(g_full.at[x_next], sem(gr_x, 1))
    send(g_full.at[x_next, half_b], g_full.at[x_next, half_b], sem(gs_x, 3), sem(gr_x, 3), left)

    @pl.when(sums_early)
    def _():
        chip_sum(early)

    alphas(12, 16)
    far_beta(2)
    far_beta(3)
    product(late)

    @pl.when(sums_early)
    def _():
        to_core(late).start()

    landed(g_full.at[x_far, half_a], sem(gr_x, 2))
    landed(g_full.at[x_far, half_b], sem(gr_x, 3))

    def transpose(q, carry):
        g_train_t[q] = g_full[q, 0:TOK_DP, :].astype(F32).T.astype(BF16)
        return carry

    lax.fori_loop(0, 4, transpose, 0)

    @pl.when(jnp.logical_not(sums_early))
    def _():
        chip_sum(late)
        finish(late)

    @pl.when(sums_early)
    def _():
        finish(early)
        landed(rot.at[late], sem(r_c2))

    @pl.when(jnp.logical_not(sums_early))
    def _():
        landed(rot.at[early], sem(r_c2))

    query_rot = jnp.concatenate([rot[0, :, TRAIN:], rot[1, :, TRAIN:]], axis=1).astype(F32)
    query_grad = jnp.concatenate([g_full[q, TOK_DP:, :] for q in range(4)], axis=0)
    for p in range(PAIRS):
        masked = jnp.where(pid[...] == p, query_rot, 0.0).astype(BF16)
        precond[p] = (jnp.dot(masked, query_grad, preferred_element_type=F32) * recip[...]).astype(BF16)

    def token_scores(q, carry):
        lanes = pl.ds(pl.multiple_of((q % 2) * TOK_DP, 128), TOK_DP)
        train = rot[q // 2, :, lanes].astype(F32)
        rows = []
        for p in range(PAIRS):
            projected = jnp.dot(precond[p], g_train_t[q], preferred_element_type=F32)
            rows.append(jnp.sum(projected * train, axis=0, keepdims=True))
        rows.append(jnp.zeros((8 - PAIRS, TOK_DP), F32))
        tok[q % 2, q // 2] = jnp.concatenate(rows, axis=0)
        return carry

    lax.fori_loop(0, 4, token_scores, 0)

    ts_c, tr_c, ts_y, tr_y = (names.take() for _ in range(4))
    send(tok.at[1 - c], tok_in, sem(ts_c), sem(tr_c), core)
    landed(tok_in, sem(tr_c))
    tok_y[...] = tok[c] + tok_in[...]
    send(tok_y.at[1 - k], tok_yin, sem(ts_y), sem(tr_y), mate)
    landed(tok_yin, sem(tr_y))
    scores = tok_y[k] + tok_yin[...]

    lane = lax.broadcasted_iota(jnp.int32, (8, TOK_DP), 1)
    column = lax.broadcasted_iota(jnp.int32, (8, 128), 1)
    result = jnp.zeros((8, 128), F32)
    start = jnp.int32(0)
    for n in range(SEQ_DP):
        end = start + lengths[0, n]
        part = jnp.sum(jnp.where((lane >= start) & (lane < end), scores, 0.0), axis=1, keepdims=True)
        result = jnp.where(column == n, part, result)
        start = end

    for buf, at, target in (
        (red_x, x, lambda o: device(x + o, y, z, c)),
        (red_z, z, lambda o: device(x, y, z + o, c)),
    ):
        s_red, r_red = names.take(3), names.take(4)
        buf[at] = result
        for i, o in enumerate(OTHER):
            send(buf.at[at], buf.at[at], sem(s_red, i), sem(r_red, at), target(o))
        for o in OTHER:
            landed(buf.at[(at + o) % 4], sem(r_red, (at + o) % 4))
        result = (buf[0] + buf[1]) + (buf[2] + buf[3])
    s_red, r_red = names.take(), names.take()
    red_y[y // 2] = result
    send(red_y.at[y // 2], red_y.at[y // 2], sem(s_red), sem(r_red), device(x, y + 2, z, c))
    landed(red_y.at[1 - y // 2], sem(r_red))
    out[...] = (red_y[0] + red_y[1]) * SCALE

    for cp in sent:
        cp.wait_send()

    @pl.when(partner_zeta == 0)
    def _():
        to_units.wait_send()

    @pl.when(partner_zeta == 2)
    def _():
        to_other.wait_send()

    @pl.when((partner_zeta == 0) | (partner_zeta == 2))
    def _():
        to_query.wait_send()

    for i in range(2):
        y_beta_other(i).wait_send()
    y_beta_own().wait_send()

    @pl.when(is_own | is_other)
    def _():
        for i in range(3):
            z_beta(i, True).wait_send()
            x_alpha(i, True).wait_send()
        for i in range(4):
            y_alpha_own(i, x).wait_send()

    @pl.when(is_other)
    def _():
        for i in range(4):
            y_alpha_other(i, x, 3).wait_send()

    def drain_x(n, carry):
        x_beta(n, x, y, 1).wait_send()
        return carry

    lax.fori_loop(0, 12, drain_x, 0)

    @pl.when(pi != 3)
    def _():
        def drain_z(t, carry):
            z_alpha(t, x, y).wait_send()
            return carry

        lax.fori_loop(0, 16, drain_z, 0)

    to_core(0).wait_send()
    to_mate().wait_send()
    back_to_core(0).wait_send()

    assert names.used <= N_SEMS


def fused(train_t, query, train_g_t, query_g, pid, lengths, in_basis_t, eig_t, out_basis):
    vmem, hbm = pl.BlockSpec(memory_space=pltpu.VMEM), pl.BlockSpec(memory_space=pl.ANY)
    smem = pl.BlockSpec(memory_space=pltpu.SMEM)

    def v(shape, dtype=BF16):
        return pltpu.VMEM(shape, dtype)

    return pl.pallas_call(
        kernel,
        out_shape=jax.ShapeDtypeStruct((8, 128), F32),
        in_specs=[vmem, vmem, vmem, vmem, vmem, smem, hbm, hbm, hbm],
        out_specs=vmem,
        scratch_shapes=[
            v((2, DEPTH, LANES)),
            v((4, COLS, LANES)),
            v((COLS, DEPTH)),
            v((2, COLS, LANES), F32),
            v((COLS, LANES - TRAIN)),
            v((COLS, LANES - TRAIN)),
            v((COLS, QUART)),
            v((COLS, QUART), F32),
            v((4, ROWS, FEAT)),
            v((4, ROWS, FEAT)),
            v((4, FEAT, QUART)),
            v((ROWS, QUART), F32),
            v((ROWS, QUART)),
            v((4, CHUNK, QUART)),
            v((CHUNK, QUART)),
            v((CHUNK, QUART)),
            v((4, ROWS, QUART)),
            v((4, QUART, TOK_DP)),
            v((COLS, LANES), F32),
            v((COLS, LANES)),
            v((COLS, LANES)),
            v((2, COLS, LANES)),
            v((PAIRS, COLS, QUART)),
            v((2, 2, 8, TOK_DP), F32),
            v((2, 8, TOK_DP), F32),
            v((2, 8, TOK_DP), F32),
            v((8, TOK_DP), F32),
            v((4, 8, 128), F32),
            v((4, 8, 128), F32),
            v((2, 8, 128), F32),
            pltpu.SemaphoreType.DMA((N_SEMS,)),
        ],
        compiler_params=pltpu.CompilerParams(
            collective_id=0, has_side_effects=True, vmem_limit_bytes=60 * 2**20
        ),
        cost_estimate=pl.CostEstimate(
            flops=2 * 1280 * 4736 * 592 + 8 * 896 * 592 * 1280, bytes_accessed=20 * 2**20, transcendentals=0
        ),
        name="influence",
    )(train_t, query, train_g_t, query_g, pid, lengths, in_basis_t, eig_t, out_basis)


def on_device(
    train_act,
    train_out_grad,
    query_act,
    query_out_grad,
    in_basis,
    out_basis,
    eigvals,
    pair_ids,
    seq_lengths,
):
    scores = fused(
        train_act.T,
        query_act,
        train_out_grad.T,
        query_out_grad,
        pair_ids[None, :],
        seq_lengths,
        in_basis.T,
        eigvals.T,
        out_basis,
    )
    return scores[:PAIRS, :SEQ_DP]


def solution(mesh):
    in_specs = (
        P("dp", "basis"),
        P("dp", "basis"),
        P("dp", "basis"),
        P("dp", "basis"),
        P("dp", "basis"),
        P("basis", None),
        P(None, "basis"),
        P(),
        P("dp", None),
    )
    out_specs = P(None, "dp")
    return jax.shard_map(
        on_device, mesh=mesh, in_specs=in_specs, out_specs=out_specs, check_vma=False
    )
```

```python
import functools
import math

import jax
import jax.numpy as jnp
from jax import lax
from jax.experimental import pallas as pl
from jax.experimental.pallas import tpu as pltpu
from jax.sharding import PartitionSpec as P

D = 3584
FF = 18944
PAIRS = 4
SEQ_DP = 4
TOK_DP = 256
QTOK_DP = 64
ROWS = TOK_DP + QTOK_DP
COLS = FF // 32
DEPTH = FF // 4
FEAT = D // 32
QUART = D // 4
LANES = 2 * ROWS
TRAIN = 2 * TOK_DP
CHUNK = ROWS // 4

DAMPING = 0.5
SCALE = SEQ_DP / math.sqrt(D * FF * TOK_DP * QTOK_DP)
MESH = pl.DeviceIdType.MESH
F32, BF16 = jnp.float32, jnp.bfloat16

RB = 368
PARTS = 2
RA = (COLS - RB) // PARTS
OTHER = (1, 3, 2)
CHUNKS = ((TRAIN, LANES - TRAIN), (0, TOK_DP), (TOK_DP, TOK_DP))
COPIES = ((0,), (1, 2), (3, 4))


def place():
    dp, b = lax.axis_index("dp"), lax.axis_index("basis")
    return b % 4, ((b // 4) % 2) * 2 + dp // 2, b // 8, dp % 2


def device(x, y, z, c):
    x, y, z = (x + 4) % 4, (y + 4) % 4, (z + 4) % 4
    return ((y % 2) * 2 + c, z * 8 + (y // 2) * 4 + x)


class Sems:
    def __init__(self):
        self.used = 0

    def take(self, n=1):
        self.used += n
        return self.used - n


N_SEMS = 256


def kernel(
    train_t, query, train_g_t, query_g, pid, lengths, w_hbm, eig_hbm, ob_hbm, out,
    units, other, w, acc, query_t, query_in, eig, recip,
    og_tok, og_feat, ob, g_sum, g_part, g_rz, g_yb, g_ry, g_full, g_train_t,
    sum_in, chip_out, chip_in, rot, precond, tok, tok_in, red_x, red_z,
    sems,
):
    x, y, z, c = place()
    k = y % 2
    d = 2 * k + c
    zeta = (z - d + 4) % 4
    sign = 1 - 2 * c
    pi = (sign * zeta + 4) % 4
    is_own, is_other = zeta == 0, zeta == 2
    names = Sems()

    def sem(base, i=0):
        return sems.at[base + i]

    def slot(xs, ys):
        return ((xs + 4) % 4) * 4 + (ys + 4) % 4

    def unit(xs, ys, low, count, lanes=None):
        xs, ys = (xs + 4) % 4, (ys + 4) % 4
        rows = pl.ds(pl.multiple_of(COLS * (4 * (ys // 2) + xs) + low, 16), count)
        return units.at[ys % 2, rows] if lanes is None else units.at[ys % 2, rows, lanes]

    def beta(xs, ys):
        return unit(xs, ys, 0, RB)

    def alpha(xs, ys, h):
        return unit(xs, ys, RB + h * RA, RA)

    def other_alpha(xs, h):
        return other.at[xs, pl.ds(RB + h * RA, RA)]

    def copy(src, dst, send, recv, target):
        return pltpu.make_async_remote_copy(
            src_ref=src, dst_ref=dst, send_sem=send, recv_sem=recv, device_id=target, device_id_type=MESH
        )

    partners = [device(x + o, y, z, c) for o in OTHER]
    partners += [device(x, y + o, z, c) for o in OTHER]
    partners += [device(x, y, z + o, c) for o in OTHER]
    core = device(x, y, z, 1 - c)
    partners += [core] + [device(x, y + o, z, 1 - c) for o in OTHER]
    mate = device(x, y + 1 - 2 * k, z, c)

    def landed(dst, recv):
        copy(dst, dst, sem(dummy), recv, core).wait_recv()

    sent = []

    def send(src, dst, s, r, target):
        cp = copy(src, dst, s, r, target)
        cp.start()
        sent.append(cp)

    dummy = names.take()
    s_w, s_eig, s_ob, s_own = names.take(), names.take(), names.take(), names.take()
    s_step, r_step = names.take(2), names.take(2)
    r_b, r_a, r_ob, r_oa = names.take(16), names.take(16 * PARTS), names.take(), names.take(4 * PARTS)
    s_zb, s_yb, s_xb = names.take(3), names.take(3), names.take(12)
    s_xa, s_ya, s_ya2, s_za = (names.take(n * PARTS) for n in (3, 4, 4, 16))

    w_copy = pltpu.make_async_copy(w_hbm, w, sem(s_w))
    w_copy.start()
    quarter = pl.ds(pl.multiple_of(d * QUART, 128), QUART)
    ob_copy = pltpu.make_async_copy(ob_hbm.at[:, quarter], ob.at[x], sem(s_ob))
    ob_copy.start()
    eig_copy = pltpu.make_async_copy(eig_hbm.at[:, quarter], eig, sem(s_eig))
    eig_copy.start()

    barrier = pltpu.get_barrier_semaphore()
    for p in partners:
        pl.semaphore_signal(barrier, inc=1, device_id=p, device_id_type=MESH)
    pl.semaphore_wait(barrier, len(partners))

    turned = query[...].astype(F32).T.astype(BF16)
    nothing = jnp.zeros_like(turned)
    query_t[...] = jnp.concatenate(
        [jnp.where(c == 0, turned, nothing), jnp.where(c == 1, turned, nothing)], axis=1
    )
    og_tok[d, 0:TOK_DP, :] = train_g_t[...].astype(F32).T.astype(BF16)
    og_tok[d, TOK_DP:, :] = query_g[...]

    gs_c, gr_c = names.take(), names.take()
    send(og_tok.at[d], og_tok.at[d], sem(gs_c), sem(gr_c), core)

    mine = pl.ds(pl.multiple_of(c * TOK_DP, 128), TOK_DP)
    theirs = pl.ds(pl.multiple_of((1 - c) * TOK_DP, 128), TOK_DP)
    tail = pl.ds(TRAIN, LANES - TRAIN)
    partner_zeta = (zeta - sign + 4) % 4
    to_units = copy(train_t, unit(x, y, 0, COLS, mine), sem(s_step), sem(r_step), core)
    to_other = copy(train_t, other.at[x, :, mine], sem(s_step), sem(r_step), core)
    to_query = copy(query_t, query_in, sem(s_step, 1), sem(r_step, 1), core)

    @pl.when(partner_zeta == 0)
    def _():
        to_units.start()

    @pl.when(partner_zeta == 2)
    def _():
        to_other.start()

    @pl.when((partner_zeta == 0) | (partner_zeta == 2))
    def _():
        to_query.start()

    def z_beta(i, own):
        piece = beta(x, y) if own else other.at[x, pl.ds(0, RB)]
        return copy(piece, piece, sem(s_zb, i), sem(r_b, slot(x, y)) if own else sem(r_ob), device(x, y, z + OTHER[i], c))

    def got_alpha(xs, ys, h):
        return sem(r_a, PARTS * slot(xs, ys) + h)

    def x_alpha(i, own, h):
        piece = alpha(x, y, h) if own else other_alpha(x, h)
        got = got_alpha(x, y, h) if own else sem(r_oa, PARTS * x + h)
        return copy(piece, piece, sem(s_xa, PARTS * i + h), got, device(x + OTHER[i], y, z, c))

    def z_alpha(t, xs, ys, h):
        piece = alpha(xs, ys, h)
        return copy(piece, piece, sem(s_za, PARTS * t + h), got_alpha(xs, ys, h), device(x, y, z + sign, c))

    def y_alpha_own(i, xs, h):
        piece = alpha(xs, y, h)
        return copy(piece, piece, sem(s_ya, PARTS * i + h), got_alpha(xs, y, h), device(x, y + 2, z, c))

    def y_alpha_other(i, xs, step, h):
        sent_by = sem(s_ya if step == 1 else s_ya2, PARTS * i + h)
        return copy(other_alpha(xs, h), alpha(xs, y, h), sent_by, got_alpha(xs, y, h), device(x, y + step, z, c))

    def y_beta_own():
        piece = beta(x, y)
        return copy(piece, piece, sem(s_yb, 2), sem(r_b, slot(x, y)), device(x, y + 2, z, c))

    def y_beta_other(i):
        src = other.at[x, pl.ds(0, RB)]
        return copy(src, beta(x, y), sem(s_yb, i), sem(r_b, slot(x, y)), device(x, y + OTHER[i], z, c))

    def x_beta(n, xs, ys, step):
        piece = beta(xs, ys)
        return copy(piece, piece, sem(s_xb, n), sem(r_b, slot(xs, ys)), device(x + step, y, z, c))

    def gather_step(dst_mine, dst_theirs, dst_tail):
        own = pltpu.make_async_copy(train_t, dst_mine, sem(s_own))
        own.start()
        own.wait()
        landed(query_in, sem(r_step, 1))
        dst_tail[...] = query_t[...] + query_in[...]
        landed(dst_theirs, sem(r_step))

    @pl.when(is_own)
    def _():
        gather_step(unit(x, y, 0, COLS, mine), unit(x, y, 0, COLS, theirs), unit(x, y, 0, COLS, tail))
        for i in range(3):
            z_beta(i, True).start()
            for h in range(PARTS):
                x_alpha(i, True, h).start()

    @pl.when(is_other)
    def _():
        gather_step(other.at[x, :, mine], other.at[x, :, theirs], other.at[x, :, tail])
        for i in range(3):
            z_beta(i, False).start()
            for h in range(PARTS):
                x_alpha(i, False, h).start()
        for h in range(PARTS):
            y_alpha_other(0, x, 1, h).start()
            y_alpha_other(0, x, 3, h).start()

    @pl.when(is_own)
    def _():
        for h in range(PARTS):
            y_alpha_own(0, x, h).start()

    gs_y, gr_y = names.take(2), names.take(2)
    landed(og_tok.at[2 * k + 1 - c], sem(gr_c))
    send(og_tok.at[2 * k], og_tok.at[2 * k], sem(gs_y), sem(gr_y), mate)
    send(og_tok.at[2 * k + 1], og_tok.at[2 * k + 1], sem(gs_y, 1), sem(gr_y, 1), mate)
    ob_copy.wait()
    gs_ob, gr_ob = names.take(3), names.take(4)
    for i, o in enumerate(OTHER):
        send(ob.at[x], ob.at[x], sem(gs_ob, i), sem(gr_ob, x), device(x + o, y, z, c))

    ALPHA = [(0, 0), (1, 0), (3, 0), (2, 0), (0, 2), (0, 1), (0, 3), (1, 2), (3, 2), (2, 2)]
    ALPHA += [(1, 1), (1, 3), (3, 1), (3, 3), (2, 1), (2, 3)]
    BETA = (0, 2, 1, 3)

    def on_x(o):
        return (x + o) % 4

    def on_y(o):
        return (y + o) % 4

    def alphas(first, last):
        for t in range(first, last):
            dx, dy = ALPHA[t]
            xs, ys = on_x(dx), on_y(dy)
            for h in range(PARTS):
                if (dx, dy) == (0, 0):

                    @pl.when(jnp.logical_not(is_own))
                    def _():
                        landed(alpha(xs, ys, h), got_alpha(xs, ys, h))
                else:
                    landed(alpha(xs, ys, h), got_alpha(xs, ys, h))

                @pl.when(pi != 3)
                def _():
                    z_alpha(t, xs, ys, h).start()

    def own_beta(i):
        ys = on_y(BETA[i])
        if i == 0:

            @pl.when(jnp.logical_not(is_own))
            def _():
                landed(beta(x, ys), sem(r_b, slot(x, ys)))
        else:
            landed(beta(x, ys), sem(r_b, slot(x, ys)))
        x_beta(2 * i, x, ys, 1).start()
        x_beta(2 * i + 1, x, ys, 3).start()

    def side_beta(i):
        ys = on_y(BETA[i])
        order = ((3, 1), (1, 3))[i % 2]
        for n, dx in enumerate(order):
            landed(beta(on_x(dx), ys), sem(r_b, slot(on_x(dx), ys)))
            if n == 0:
                x_beta(8 + i, on_x(dx), ys, 4 - dx).start()

    def far_beta(i):
        ys = on_y(BETA[i])
        landed(beta(on_x(2), ys), sem(r_b, slot(on_x(2), ys)))

    own_beta(0)
    y_beta_own().start()

    @pl.when(jnp.logical_not(is_other))
    def _():
        landed(other.at[x, pl.ds(0, RB)], sem(r_ob))

    y_beta_other(0).start()
    y_beta_other(1).start()
    alphas(0, 2)

    landed(og_tok.at[2 * (1 - k)], sem(gr_y))
    landed(og_tok.at[2 * (1 - k) + 1], sem(gr_y, 1))
    gs_f, gr_f = names.take(3), names.take(4)
    for i, o in enumerate(OTHER):
        q = (x + o) % 4
        send(og_tok.at[q], og_feat.at[x], sem(gs_f, i), sem(gr_f, x), device(x + o, y, z, c))
    og_feat[x] = og_tok[x]

    own_beta(1)
    alphas(2, 4)

    side_beta(0)
    for o in OTHER:
        xs = (x + o) % 4
        landed(og_feat.at[xs], sem(gr_f, xs))
        landed(ob.at[xs], sem(gr_ob, xs))

    def feature_block(i, carry):
        g_sum[...] += jnp.dot(og_feat[i], ob[i], preferred_element_type=F32)
        return carry

    g_sum[...] = jnp.zeros_like(g_sum)
    lax.fori_loop(0, 4, feature_block, 0)
    g_part[...] = g_sum[...].astype(BF16)

    def chunk(zz):
        return pl.ds(pl.multiple_of(((zz + 4) % 4) * CHUNK, 16), CHUNK)

    gs_z, gr_z = names.take(3), names.take(4)
    for i, o in enumerate(OTHER):
        send(g_part.at[chunk(z + o)], g_rz.at[z], sem(gs_z, i), sem(gr_z, z), device(x, y, z + o, c))

    eig_copy.wait()
    recip[...] = 1.0 / (eig[...].astype(F32) + DAMPING)

    own_beta(2)
    own_beta(3)

    @pl.when(is_own)
    def _():
        for i, dx in enumerate(OTHER):
            for h in range(PARTS):
                y_alpha_own(i + 1, on_x(dx), h).start()

    @pl.when(is_other)
    def _():
        for i, dx in enumerate(OTHER):
            for h in range(PARTS):
                landed(other_alpha(on_x(dx), h), sem(r_oa, PARTS * on_x(dx) + h))
                y_alpha_other(i + 1, on_x(dx), 1, h).start()
                y_alpha_other(i + 1, on_x(dx), 3, h).start()

    alphas(4, 5)
    side_beta(1)
    alphas(5, 6)
    total = g_sum[chunk(z), :]
    for o in OTHER:
        zz = (z + o) % 4
        landed(g_rz.at[zz], sem(gr_z, zz))
        total = total + g_rz[zz].astype(F32)
    g_sum[chunk(z), :] = total
    g_yb[...] = total.astype(BF16)
    gs_h, gr_h = names.take(), names.take()
    send(g_yb, g_ry, sem(gs_h), sem(gr_h), device(x, y + 2, z, c))

    alphas(6, 8)
    landed(g_ry, sem(gr_h))
    g_full[x, chunk(z), :] = (g_sum[chunk(z), :] + g_ry[...].astype(F32)).astype(BF16)
    gs_g, gr_g = names.take(3), names.take(4)
    for i, o in enumerate(OTHER):
        piece = g_full.at[x, chunk(z)]
        send(piece, piece, sem(gs_g, i), sem(gr_g, z), device(x, y, z + o, c))

    side_beta(2)
    alphas(8, 9)
    for o in OTHER:
        zz = (z + o) % 4
        landed(g_full.at[x, chunk(zz)], sem(gr_g, zz))
    gs_x, gr_x, gs_v, gr_v = names.take(3), names.take(4), names.take(3), names.take(4)

    def rows_of(yh):
        return pl.ds(pl.multiple_of(yh * (ROWS // 2), 16), ROWS // 2)

    low, high = rows_of(y // 2), rows_of(1 - y // 2)
    for i, o in enumerate(OTHER):
        send(g_full.at[x, low], g_full.at[x, low], sem(gs_x, i), sem(gr_x, x), device(x + o, y, z, c))

    alphas(9, 10)
    far_beta(0)
    far_beta(1)
    w_copy.wait()

    def lanes(n):
        return pl.ds(*CHUNKS[n])

    def product(yl, n):
        ln = lanes(n)
        acc[yl, :, ln] = jnp.dot(w[:, 4608:], units[yl, 4608:, ln], preferred_element_type=F32)

        def body(i, carry):
            rows = pl.ds(pl.multiple_of(i * 768, 128), 768)
            acc[yl, :, ln] += jnp.dot(w[:, rows], units[yl, rows, ln], preferred_element_type=F32)
            return carry

        lax.fori_loop(0, 6, body, 0)

    s_c1, r_c1, s_m, r_m, s_c2, r_c2 = (names.take(n) for n in (3, 3, 5, 5, 3, 3))
    early, late = k, 1 - k
    sums_early = c == early
    sums_late = jnp.logical_not(sums_early)

    def along_y(m):
        return pl.ds(((m + 4) % 5) * 128, 128)

    def to_core(yl, n):
        return copy(acc.at[yl, :, lanes(n)], sum_in.at[:, lanes(n)], sem(s_c1, n), sem(r_c1, n), core)

    def to_mate(m):
        return copy(chip_out.at[:, along_y(m)], chip_in.at[:, along_y(m)], sem(s_m, m), sem(r_m, m), mate)

    def back_to_core(yl, n):
        piece = rot.at[yl, :, lanes(n)]
        return copy(piece, piece, sem(s_c2, n), sem(r_c2, n), core)

    def chip_sum(yl, n):
        ln = lanes(n)
        landed(sum_in.at[:, ln], sem(r_c1, n))
        total = acc[yl, :, ln] + sum_in[:, ln]
        acc[yl, :, ln] = total
        chip_out[:, ln] = total.astype(BF16)
        for m in COPIES[n]:
            to_mate(m).start()

    def finish(yl, n):
        ln = lanes(n)
        for m in COPIES[n]:
            landed(chip_in.at[:, along_y(m)], sem(r_m, m))
        rot[yl, :, ln] = (acc[yl, :, ln] + chip_in[:, ln].astype(F32)).astype(BF16)
        back_to_core(yl, n).start()

    for n in range(3):
        product(early, n)

        @pl.when(sums_late)
        def _():
            to_core(early, n).start()

    alphas(10, 12)
    side_beta(3)
    for i, o in enumerate(OTHER):
        q = on_x(o)
        landed(g_full.at[q, low], sem(gr_x, q))
        send(g_full.at[q, low], g_full.at[q, low], sem(gs_v, i), sem(gr_v, q), device(x, y + 2, z, c))

    @pl.when(sums_early)
    def _():
        for n in range(3):
            chip_sum(early, n)

    alphas(12, 16)
    far_beta(2)
    far_beta(3)
    def late_product(n):
        product(late, n)

        @pl.when(sums_early)
        def _():
            to_core(late, n).start()

    def late_sum(n):
        @pl.when(sums_late)
        def _():
            chip_sum(late, n)
            finish(late, n)

    late_product(0)
    late_product(1)
    late_sum(0)
    late_product(2)
    late_sum(1)
    late_sum(2)

    for o in OTHER:
        landed(g_full.at[on_x(o), high], sem(gr_v, on_x(o)))

    def transpose(q, carry):
        g_train_t[q] = g_full[q, 0:TOK_DP, :].astype(F32).T.astype(BF16)
        return carry

    lax.fori_loop(0, 4, transpose, 0)

    def finish_early(n):
        @pl.when(sums_early)
        def _():
            finish(early, n)

    def await_early(n):
        @pl.when(sums_late)
        def _():
            landed(rot.at[early, :, lanes(n)], sem(r_c2, n))

    def await_late(n):
        @pl.when(sums_early)
        def _():
            landed(rot.at[late, :, lanes(n)], sem(r_c2, n))

    finish_early(0)
    await_early(0)
    await_late(0)

    query_rot = jnp.concatenate([rot[0, :, TRAIN:], rot[1, :, TRAIN:]], axis=1).astype(F32)
    query_grad = jnp.concatenate([g_full[q, TOK_DP:, :] for q in range(4)], axis=0)
    for p in range(PAIRS):
        masked = jnp.where(pid[...] == p, query_rot, 0.0).astype(BF16)
        precond[p] = (jnp.dot(masked, query_grad, preferred_element_type=F32) * recip[...]).astype(BF16)

    def token_scores(yl, cc):
        train = rot[yl, :, lanes(1 + cc)].astype(F32)
        rows = []
        for p in range(PAIRS):
            projected = jnp.dot(precond[p], g_train_t[2 * yl + cc], preferred_element_type=F32)
            rows.append(jnp.sum(projected * train, axis=0, keepdims=True))
        rows.append(jnp.zeros((8 - PAIRS, TOK_DP), F32))
        tok[cc, yl] = jnp.concatenate(rows, axis=0)

    finish_early(1)
    await_late(1)
    token_scores(late, 0)
    finish_early(2)
    await_late(2)
    token_scores(late, 1)
    await_early(1)
    token_scores(early, 0)
    await_early(2)
    token_scores(early, 1)

    ts, tr = names.take(7), names.take(8)
    own_slot = 2 * y + c
    tok_in[own_slot] = tok[c, k]
    to = [(o, cc) for o in (0, 1, 3, 2) for cc in (0, 1)][1:]
    for i, (o, cc) in enumerate(to):
        src = tok.at[(c + cc) % 2, (k + o) % 2]
        send(src, tok_in.at[own_slot], sem(ts, i), sem(tr, own_slot), device(x, y + o, z, (c + cc) % 2))
    for o, cc in to:
        at = 2 * on_y(o) + (c + cc) % 2
        landed(tok_in.at[at], sem(tr, at))
    scores = tok_in[0]
    for i in range(1, 8):
        scores = scores + tok_in[i]

    lane = lax.broadcasted_iota(jnp.int32, (8, TOK_DP), 1)
    column = lax.broadcasted_iota(jnp.int32, (8, 128), 1)
    result = jnp.zeros((8, 128), F32)
    start = jnp.int32(0)
    for n in range(SEQ_DP):
        end = start + lengths[0, n]
        part = jnp.sum(jnp.where((lane >= start) & (lane < end), scores, 0.0), axis=1, keepdims=True)
        result = jnp.where(column == n, part, result)
        start = end

    for buf, at, target in (
        (red_x, x, lambda o: device(x + o, y, z, c)),
        (red_z, z, lambda o: device(x, y, z + o, c)),
    ):
        s_red, r_red = names.take(3), names.take(4)
        buf[at] = result
        for i, o in enumerate(OTHER):
            send(buf.at[at], buf.at[at], sem(s_red, i), sem(r_red, at), target(o))
        for o in OTHER:
            landed(buf.at[(at + o) % 4], sem(r_red, (at + o) % 4))
        result = (buf[0] + buf[1]) + (buf[2] + buf[3])
    out[...] = result * SCALE

    for cp in sent:
        cp.wait_send()

    @pl.when(partner_zeta == 0)
    def _():
        to_units.wait_send()

    @pl.when(partner_zeta == 2)
    def _():
        to_other.wait_send()

    @pl.when((partner_zeta == 0) | (partner_zeta == 2))
    def _():
        to_query.wait_send()

    for i in range(2):
        y_beta_other(i).wait_send()
    y_beta_own().wait_send()

    @pl.when(is_own | is_other)
    def _():
        for i in range(3):
            z_beta(i, True).wait_send()
            for h in range(PARTS):
                x_alpha(i, True, h).wait_send()
        for i in range(4):
            for h in range(PARTS):
                y_alpha_own(i, x, h).wait_send()

    @pl.when(is_other)
    def _():
        for i in range(4):
            for h in range(PARTS):
                y_alpha_other(i, x, 3, h).wait_send()

    def drain_x(n, carry):
        x_beta(n, x, y, 1).wait_send()
        return carry

    lax.fori_loop(0, 12, drain_x, 0)

    @pl.when(pi != 3)
    def _():
        def drain_z(t, carry):
            for h in range(PARTS):
                z_alpha(t, x, y, h).wait_send()
            return carry

        lax.fori_loop(0, 16, drain_z, 0)

    for n in range(3):
        to_core(0, n).wait_send()
        back_to_core(0, n).wait_send()
    for m in range(5):
        to_mate(m).wait_send()

    assert names.used <= N_SEMS


def fused(train_t, query, train_g_t, query_g, pid, lengths, in_basis_t, eig_t, out_basis):
    vmem, hbm = pl.BlockSpec(memory_space=pltpu.VMEM), pl.BlockSpec(memory_space=pl.ANY)
    smem = pl.BlockSpec(memory_space=pltpu.SMEM)

    def v(shape, dtype=BF16):
        return pltpu.VMEM(shape, dtype)

    return pl.pallas_call(
        kernel,
        out_shape=jax.ShapeDtypeStruct((8, 128), F32),
        in_specs=[vmem, vmem, vmem, vmem, vmem, smem, hbm, hbm, hbm],
        out_specs=vmem,
        scratch_shapes=[
            v((2, DEPTH, LANES)),
            v((4, COLS, LANES)),
            v((COLS, DEPTH)),
            v((2, COLS, LANES), F32),
            v((COLS, LANES - TRAIN)),
            v((COLS, LANES - TRAIN)),
            v((COLS, QUART)),
            v((COLS, QUART), F32),
            v((4, ROWS, FEAT)),
            v((4, ROWS, FEAT)),
            v((4, FEAT, QUART)),
            v((ROWS, QUART), F32),
            v((ROWS, QUART)),
            v((4, CHUNK, QUART)),
            v((CHUNK, QUART)),
            v((CHUNK, QUART)),
            v((4, ROWS, QUART)),
            v((4, QUART, TOK_DP)),
            v((COLS, LANES), F32),
            v((COLS, LANES)),
            v((COLS, LANES)),
            v((2, COLS, LANES)),
            v((PAIRS, COLS, QUART)),
            v((2, 2, 8, TOK_DP), F32),
            v((8, 8, TOK_DP), F32),
            v((4, 8, 128), F32),
            v((4, 8, 128), F32),
            pltpu.SemaphoreType.DMA((N_SEMS,)),
        ],
        compiler_params=pltpu.CompilerParams(
            collective_id=0, has_side_effects=True, vmem_limit_bytes=60 * 2**20
        ),
        cost_estimate=pl.CostEstimate(
            flops=2 * 1280 * 4736 * 592 + 8 * 896 * 592 * 1280, bytes_accessed=20 * 2**20, transcendentals=0
        ),
        name="influence",
    )(train_t, query, train_g_t, query_g, pid, lengths, in_basis_t, eig_t, out_basis)


def on_device(
    train_act,
    train_out_grad,
    query_act,
    query_out_grad,
    in_basis,
    out_basis,
    eigvals,
    pair_ids,
    seq_lengths,
):
    scores = fused(
        train_act.T,
        query_act,
        train_out_grad.T,
        query_out_grad,
        pair_ids[None, :],
        seq_lengths,
        in_basis.T,
        eigvals.T,
        out_basis,
    )
    return scores[:PAIRS, :SEQ_DP]


def solution(mesh):
    in_specs = (
        P("dp", "basis"),
        P("dp", "basis"),
        P("dp", "basis"),
        P("dp", "basis"),
        P("dp", "basis"),
        P("basis", None),
        P(None, "basis"),
        P(),
        P("dp", None),
    )
    out_specs = P(None, "dp")
    return jax.shard_map(
        on_device, mesh=mesh, in_specs=in_specs, out_specs=out_specs, check_vma=False
    )
```

```python
import functools
import math

import jax
import jax.numpy as jnp
from jax import lax
from jax.experimental import pallas as pl
from jax.experimental.pallas import tpu as pltpu
from jax.sharding import PartitionSpec as P

D = 3584
FF = 18944
PAIRS = 4
SEQ_DP = 4
TOK_DP = 256
QTOK_DP = 64
ROWS = TOK_DP + QTOK_DP
COLS = FF // 32
DEPTH = FF // 4
FEAT = D // 32
QUART = D // 4
LANES = 2 * ROWS
TRAIN = 2 * TOK_DP
CHUNK = ROWS // 4

DAMPING = 0.5
SCALE = SEQ_DP / math.sqrt(D * FF * TOK_DP * QTOK_DP)
MESH = pl.DeviceIdType.MESH
F32, BF16 = jnp.float32, jnp.bfloat16

RB = 368
PARTS = 2
RA = (COLS - RB) // PARTS
OTHER = (1, 3, 2)
CHUNKS = ((TRAIN, LANES - TRAIN), (0, TOK_DP), (TOK_DP, TOK_DP))
COPIES = ((0,), (1, 2), (3, 4))


def place():
    dp, b = lax.axis_index("dp"), lax.axis_index("basis")
    return b % 4, ((b // 4) % 2) * 2 + dp // 2, b // 8, dp % 2


def device(x, y, z, c):
    x, y, z = (x + 4) % 4, (y + 4) % 4, (z + 4) % 4
    return ((y % 2) * 2 + c, z * 8 + (y // 2) * 4 + x)


class Sems:
    def __init__(self):
        self.used = 0

    def take(self, n=1):
        self.used += n
        return self.used - n


N_SEMS = 320


def kernel(
    train_t, query, train_g_t, query_g, pid, lengths, w_hbm, eig_hbm, ob_hbm, out,
    units, other, w, acc, query_t, query_in, eig, recip,
    og_tok, og_feat, ob, g_sum, g_part, g_rz, g_yb, g_ry, g_full, g_train_t,
    sum_in, chip_out, chip_in, rot, precond, tok, tok_in, red,
    sems,
):
    x, y, z, c = place()
    k = y % 2
    d = 2 * k + c
    zeta = (z - d + 4) % 4
    sign = 1 - 2 * c
    pi = (sign * zeta + 4) % 4
    is_own, is_other = zeta == 0, zeta == 2
    names = Sems()

    def sem(base, i=0):
        return sems.at[base + i]

    def slot(xs, ys):
        return ((xs + 4) % 4) * 4 + (ys + 4) % 4

    def unit(xs, ys, low, count, lanes=None):
        xs, ys = (xs + 4) % 4, (ys + 4) % 4
        rows = pl.ds(pl.multiple_of(COLS * (4 * (ys // 2) + xs) + low, 16), count)
        return units.at[ys % 2, rows] if lanes is None else units.at[ys % 2, rows, lanes]

    def beta(xs, ys):
        return unit(xs, ys, 0, RB)

    def alpha(xs, ys, h):
        return unit(xs, ys, RB + h * RA, RA)

    def other_alpha(xs, h):
        return other.at[xs, pl.ds(RB + h * RA, RA)]

    def copy(src, dst, send, recv, target):
        return pltpu.make_async_remote_copy(
            src_ref=src, dst_ref=dst, send_sem=send, recv_sem=recv, device_id=target, device_id_type=MESH
        )

    partners = [device(x + o, y, z, c) for o in OTHER]
    partners += [device(x, y + o, z, c) for o in OTHER]
    partners += [device(x, y, z + o, c) for o in OTHER]
    core = device(x, y, z, 1 - c)
    partners += [core] + [device(x, y + o, z, 1 - c) for o in OTHER]
    partners += [device(x + ox, y, z + oz, c) for ox in OTHER for oz in OTHER]
    mate = device(x, y + 1 - 2 * k, z, c)

    def landed(dst, recv):
        copy(dst, dst, sem(dummy), recv, core).wait_recv()

    sent = []

    def send(src, dst, s, r, target):
        cp = copy(src, dst, s, r, target)
        cp.start()
        sent.append(cp)

    dummy = names.take()
    s_w, s_eig, s_ob, s_own = names.take(), names.take(), names.take(), names.take()
    s_step, r_step = names.take(2), names.take(2)
    r_b, r_a, r_ob, r_oa = names.take(16), names.take(16 * PARTS), names.take(), names.take(4 * PARTS)
    s_zb, s_yb, s_xb = names.take(3), names.take(3), names.take(12)
    s_xa, s_ya, s_ya2, s_za = (names.take(n * PARTS) for n in (3, 4, 4, 16))

    w_copy = pltpu.make_async_copy(w_hbm, w, sem(s_w))
    w_copy.start()
    quarter = pl.ds(pl.multiple_of(d * QUART, 128), QUART)
    ob_copy = pltpu.make_async_copy(ob_hbm.at[:, quarter], ob.at[x], sem(s_ob))
    ob_copy.start()
    eig_copy = pltpu.make_async_copy(eig_hbm.at[:, quarter], eig, sem(s_eig))
    eig_copy.start()

    turned = query[...].astype(F32).T.astype(BF16)
    nothing = jnp.zeros_like(turned)
    query_t[...] = jnp.concatenate(
        [jnp.where(c == 0, turned, nothing), jnp.where(c == 1, turned, nothing)], axis=1
    )
    og_tok[d, 0:TOK_DP, :] = train_g_t[...].astype(F32).T.astype(BF16)
    og_tok[d, TOK_DP:, :] = query_g[...]

    barrier = pltpu.get_barrier_semaphore()
    for p in partners:
        pl.semaphore_signal(barrier, inc=1, device_id=p, device_id_type=MESH)
    pl.semaphore_wait(barrier, len(partners))

    gs_c, gr_c = names.take(), names.take()
    send(og_tok.at[d], og_tok.at[d], sem(gs_c), sem(gr_c), core)

    mine = pl.ds(pl.multiple_of(c * TOK_DP, 128), TOK_DP)
    theirs = pl.ds(pl.multiple_of((1 - c) * TOK_DP, 128), TOK_DP)
    tail = pl.ds(TRAIN, LANES - TRAIN)
    partner_zeta = (zeta - sign + 4) % 4
    to_units = copy(train_t, unit(x, y, 0, COLS, mine), sem(s_step), sem(r_step), core)
    to_other = copy(train_t, other.at[x, :, mine], sem(s_step), sem(r_step), core)
    to_query = copy(query_t, query_in, sem(s_step, 1), sem(r_step, 1), core)

    @pl.when(partner_zeta == 0)
    def _():
        to_units.start()

    @pl.when(partner_zeta == 2)
    def _():
        to_other.start()

    @pl.when((partner_zeta == 0) | (partner_zeta == 2))
    def _():
        to_query.start()

    def z_beta(i, own):
        piece = beta(x, y) if own else other.at[x, pl.ds(0, RB)]
        return copy(piece, piece, sem(s_zb, i), sem(r_b, slot(x, y)) if own else sem(r_ob), device(x, y, z + OTHER[i], c))

    def got_alpha(xs, ys, h):
        return sem(r_a, PARTS * slot(xs, ys) + h)

    def x_alpha(i, own, h):
        piece = alpha(x, y, h) if own else other_alpha(x, h)
        got = got_alpha(x, y, h) if own else sem(r_oa, PARTS * x + h)
        return copy(piece, piece, sem(s_xa, PARTS * i + h), got, device(x + OTHER[i], y, z, c))

    def z_alpha(t, xs, ys, h):
        piece = alpha(xs, ys, h)
        return copy(piece, piece, sem(s_za, PARTS * t + h), got_alpha(xs, ys, h), device(x, y, z + sign, c))

    def y_alpha_own(i, xs, h):
        piece = alpha(xs, y, h)
        return copy(piece, piece, sem(s_ya, PARTS * i + h), got_alpha(xs, y, h), device(x, y + 2, z, c))

    def y_alpha_other(i, xs, step, h):
        sent_by = sem(s_ya if step == 1 else s_ya2, PARTS * i + h)
        return copy(other_alpha(xs, h), alpha(xs, y, h), sent_by, got_alpha(xs, y, h), device(x, y + step, z, c))

    def y_beta_own():
        piece = beta(x, y)
        return copy(piece, piece, sem(s_yb, 2), sem(r_b, slot(x, y)), device(x, y + 2, z, c))

    def y_beta_other(i):
        src = other.at[x, pl.ds(0, RB)]
        return copy(src, beta(x, y), sem(s_yb, i), sem(r_b, slot(x, y)), device(x, y + OTHER[i], z, c))

    def x_beta(n, xs, ys, step):
        piece = beta(xs, ys)
        return copy(piece, piece, sem(s_xb, n), sem(r_b, slot(xs, ys)), device(x + step, y, z, c))

    def gather_step(dst_mine, dst_theirs, dst_tail):
        own = pltpu.make_async_copy(train_t, dst_mine, sem(s_own))
        own.start()
        own.wait()
        landed(query_in, sem(r_step, 1))
        dst_tail[...] = query_t[...] + query_in[...]
        landed(dst_theirs, sem(r_step))

    @pl.when(is_own)
    def _():
        gather_step(unit(x, y, 0, COLS, mine), unit(x, y, 0, COLS, theirs), unit(x, y, 0, COLS, tail))
        for i in range(3):
            z_beta(i, True).start()
            for h in range(PARTS):
                x_alpha(i, True, h).start()

    @pl.when(is_other)
    def _():
        gather_step(other.at[x, :, mine], other.at[x, :, theirs], other.at[x, :, tail])
        for i in range(3):
            z_beta(i, False).start()
            for h in range(PARTS):
                x_alpha(i, False, h).start()
        for h in range(PARTS):
            y_alpha_other(0, x, 1, h).start()
            y_alpha_other(0, x, 3, h).start()

    @pl.when(is_own)
    def _():
        for h in range(PARTS):
            y_alpha_own(0, x, h).start()

    gs_y, gr_y = names.take(2), names.take(2)
    landed(og_tok.at[2 * k + 1 - c], sem(gr_c))
    send(og_tok.at[2 * k], og_tok.at[2 * k], sem(gs_y), sem(gr_y), mate)
    send(og_tok.at[2 * k + 1], og_tok.at[2 * k + 1], sem(gs_y, 1), sem(gr_y, 1), mate)
    ob_copy.wait()
    gs_ob, gr_ob = names.take(3), names.take(4)
    for i, o in enumerate(OTHER):
        send(ob.at[x], ob.at[x], sem(gs_ob, i), sem(gr_ob, x), device(x + o, y, z, c))

    ALPHA = [(0, 0), (1, 0), (3, 0), (2, 0), (0, 2), (0, 1), (0, 3), (1, 2), (3, 2), (2, 2)]
    ALPHA += [(1, 1), (1, 3), (3, 1), (3, 3), (2, 1), (2, 3)]
    BETA = (0, 2, 1, 3)

    def on_x(o):
        return (x + o) % 4

    def on_y(o):
        return (y + o) % 4

    def alphas(first, last):
        for t in range(first, last):
            dx, dy = ALPHA[t]
            xs, ys = on_x(dx), on_y(dy)
            for h in range(PARTS):
                if (dx, dy) == (0, 0):

                    @pl.when(jnp.logical_not(is_own))
                    def _():
                        landed(alpha(xs, ys, h), got_alpha(xs, ys, h))
                else:
                    landed(alpha(xs, ys, h), got_alpha(xs, ys, h))

                @pl.when(pi != 3)
                def _():
                    z_alpha(t, xs, ys, h).start()

    def own_beta(i):
        ys = on_y(BETA[i])
        if i == 0:

            @pl.when(jnp.logical_not(is_own))
            def _():
                landed(beta(x, ys), sem(r_b, slot(x, ys)))
        else:
            landed(beta(x, ys), sem(r_b, slot(x, ys)))
        x_beta(2 * i, x, ys, 1).start()
        x_beta(2 * i + 1, x, ys, 3).start()

    def side_beta(i):
        ys = on_y(BETA[i])
        order = ((3, 1), (1, 3))[i % 2]
        for n, dx in enumerate(order):
            landed(beta(on_x(dx), ys), sem(r_b, slot(on_x(dx), ys)))
            if n == 0:
                x_beta(8 + i, on_x(dx), ys, 4 - dx).start()

    def far_beta(i):
        ys = on_y(BETA[i])
        landed(beta(on_x(2), ys), sem(r_b, slot(on_x(2), ys)))

    own_beta(0)
    y_beta_own().start()

    @pl.when(jnp.logical_not(is_other))
    def _():
        landed(other.at[x, pl.ds(0, RB)], sem(r_ob))

    y_beta_other(0).start()
    y_beta_other(1).start()
    alphas(0, 2)

    landed(og_tok.at[2 * (1 - k)], sem(gr_y))
    landed(og_tok.at[2 * (1 - k) + 1], sem(gr_y, 1))
    gs_f, gr_f = names.take(3), names.take(4)
    for i, o in enumerate(OTHER):
        q = (x + o) % 4
        send(og_tok.at[q], og_feat.at[x], sem(gs_f, i), sem(gr_f, x), device(x + o, y, z, c))
    og_feat[x] = og_tok[x]

    own_beta(1)
    alphas(2, 4)

    for o in OTHER:
        xs = (x + o) % 4
        landed(og_feat.at[xs], sem(gr_f, xs))
        landed(ob.at[xs], sem(gr_ob, xs))

    def feature_block(i, carry):
        g_sum[...] += jnp.dot(og_feat[i], ob[i], preferred_element_type=F32)
        return carry

    g_sum[...] = jnp.zeros_like(g_sum)
    lax.fori_loop(0, 4, feature_block, 0)
    g_part[...] = g_sum[...].astype(BF16)

    def chunk(zz):
        return pl.ds(pl.multiple_of(((zz + 4) % 4) * CHUNK, 16), CHUNK)

    gs_z, gr_z = names.take(3), names.take(4)
    for i, o in enumerate(OTHER):
        send(g_part.at[chunk(z + o)], g_rz.at[z], sem(gs_z, i), sem(gr_z, z), device(x, y, z + o, c))

    side_beta(0)
    eig_copy.wait()
    recip[...] = 1.0 / (eig[...].astype(F32) + DAMPING)

    own_beta(2)
    own_beta(3)

    @pl.when(is_own)
    def _():
        for i, dx in enumerate(OTHER):
            for h in range(PARTS):
                y_alpha_own(i + 1, on_x(dx), h).start()

    @pl.when(is_other)
    def _():
        for i, dx in enumerate(OTHER):
            for h in range(PARTS):
                landed(other_alpha(on_x(dx), h), sem(r_oa, PARTS * on_x(dx) + h))
                y_alpha_other(i + 1, on_x(dx), 1, h).start()
                y_alpha_other(i + 1, on_x(dx), 3, h).start()

    alphas(4, 5)
    total = g_sum[chunk(z), :]
    for o in OTHER:
        zz = (z + o) % 4
        landed(g_rz.at[zz], sem(gr_z, zz))
        total = total + g_rz[zz].astype(F32)
    g_sum[chunk(z), :] = total
    g_yb[...] = total.astype(BF16)
    gs_h, gr_h = names.take(), names.take()
    send(g_yb, g_ry, sem(gs_h), sem(gr_h), device(x, y + 2, z, c))

    side_beta(1)
    alphas(5, 6)
    landed(g_ry, sem(gr_h))
    g_full[x, chunk(z), :] = (g_sum[chunk(z), :] + g_ry[...].astype(F32)).astype(BF16)
    gs_g, gr_g = names.take(3), names.take(4)
    for i, o in enumerate(OTHER):
        piece = g_full.at[x, chunk(z)]
        send(piece, piece, sem(gs_g, i), sem(gr_g, z), device(x, y, z + o, c))

    alphas(6, 8)
    side_beta(2)
    alphas(8, 9)
    for o in OTHER:
        zz = (z + o) % 4
        landed(g_full.at[x, chunk(zz)], sem(gr_g, zz))
    gs_x, gr_x, gs_v, gr_v = names.take(3), names.take(4), names.take(3), names.take(4)

    def rows_of(yh):
        return pl.ds(pl.multiple_of(yh * (ROWS // 2), 16), ROWS // 2)

    low, high = rows_of(y // 2), rows_of(1 - y // 2)
    for i, o in enumerate(OTHER):
        send(g_full.at[x, low], g_full.at[x, low], sem(gs_x, i), sem(gr_x, x), device(x + o, y, z, c))

    alphas(9, 10)
    far_beta(0)
    far_beta(1)
    w_copy.wait()

    def lanes(n):
        return pl.ds(*CHUNKS[n])

    def product(yl, n):
        ln = lanes(n)
        acc[yl, :, ln] = jnp.dot(w[:, 4608:], units[yl, 4608:, ln], preferred_element_type=F32)

        def body(i, carry):
            rows = pl.ds(pl.multiple_of(i * 768, 128), 768)
            acc[yl, :, ln] += jnp.dot(w[:, rows], units[yl, rows, ln], preferred_element_type=F32)
            return carry

        lax.fori_loop(0, 6, body, 0)

    s_c1, r_c1, s_m, r_m, s_c2, r_c2 = (names.take(n) for n in (3, 3, 5, 5, 3, 3))
    early, late = k, 1 - k
    sums_early = c == early
    sums_late = jnp.logical_not(sums_early)

    def along_y(m):
        return pl.ds(((m + 4) % 5) * 128, 128)

    def to_core(yl, n):
        return copy(acc.at[yl, :, lanes(n)], sum_in.at[:, lanes(n)], sem(s_c1, n), sem(r_c1, n), core)

    def to_mate(m):
        return copy(chip_out.at[:, along_y(m)], chip_in.at[:, along_y(m)], sem(s_m, m), sem(r_m, m), mate)

    def back_to_core(yl, n):
        piece = rot.at[yl, :, lanes(n)]
        return copy(piece, piece, sem(s_c2, n), sem(r_c2, n), core)

    def chip_sum(yl, n):
        ln = lanes(n)
        landed(sum_in.at[:, ln], sem(r_c1, n))
        total = acc[yl, :, ln] + sum_in[:, ln]
        acc[yl, :, ln] = total
        chip_out[:, ln] = total.astype(BF16)
        for m in COPIES[n]:
            to_mate(m).start()

    def finish(yl, n):
        ln = lanes(n)
        for m in COPIES[n]:
            landed(chip_in.at[:, along_y(m)], sem(r_m, m))
        rot[yl, :, ln] = (acc[yl, :, ln] + chip_in[:, ln].astype(F32)).astype(BF16)
        back_to_core(yl, n).start()

    for n in range(3):
        product(early, n)

        @pl.when(sums_late)
        def _():
            to_core(early, n).start()

    alphas(10, 12)
    side_beta(3)
    for i, o in enumerate(OTHER):
        q = on_x(o)
        landed(g_full.at[q, low], sem(gr_x, q))
        send(g_full.at[q, low], g_full.at[q, low], sem(gs_v, i), sem(gr_v, q), device(x, y + 2, z, c))

    @pl.when(sums_early)
    def _():
        for n in range(3):
            chip_sum(early, n)

    alphas(12, 16)
    far_beta(2)
    far_beta(3)
    def late_product(n):
        product(late, n)

        @pl.when(sums_early)
        def _():
            to_core(late, n).start()

    def late_sum(n):
        @pl.when(sums_late)
        def _():
            chip_sum(late, n)
            finish(late, n)

    late_product(0)
    late_product(1)
    late_sum(0)
    late_product(2)
    late_sum(1)
    late_sum(2)

    for o in OTHER:
        landed(g_full.at[on_x(o), high], sem(gr_v, on_x(o)))

    def transpose(q, carry):
        g_train_t[q] = g_full[q, 0:TOK_DP, :].astype(F32).T.astype(BF16)
        return carry

    lax.fori_loop(0, 4, transpose, 0)

    def finish_early(n):
        @pl.when(sums_early)
        def _():
            finish(early, n)

    def await_early(n):
        @pl.when(sums_late)
        def _():
            landed(rot.at[early, :, lanes(n)], sem(r_c2, n))

    def await_late(n):
        @pl.when(sums_early)
        def _():
            landed(rot.at[late, :, lanes(n)], sem(r_c2, n))

    finish_early(0)
    await_early(0)
    await_late(0)

    query_rot = jnp.concatenate([rot[0, :, TRAIN:], rot[1, :, TRAIN:]], axis=1).astype(F32)
    query_grad = jnp.concatenate([g_full[q, TOK_DP:, :] for q in range(4)], axis=0)
    for p in range(PAIRS):
        masked = jnp.where(pid[...] == p, query_rot, 0.0).astype(BF16)
        precond[p] = (jnp.dot(masked, query_grad, preferred_element_type=F32) * recip[...]).astype(BF16)

    def token_scores(yl, cc):
        train = rot[yl, :, lanes(1 + cc)].astype(F32)
        rows = []
        for p in range(PAIRS):
            projected = jnp.dot(precond[p], g_train_t[2 * yl + cc], preferred_element_type=F32)
            rows.append(jnp.sum(projected * train, axis=0, keepdims=True))
        rows.append(jnp.zeros((8 - PAIRS, TOK_DP), F32))
        tok[cc, yl] = jnp.concatenate(rows, axis=0)

    finish_early(1)
    await_late(1)
    token_scores(late, 0)
    finish_early(2)
    await_late(2)
    token_scores(late, 1)
    await_early(1)
    token_scores(early, 0)
    await_early(2)
    token_scores(early, 1)

    ts, tr = names.take(7), names.take(8)
    own_slot = 2 * y + c
    tok_in[own_slot] = tok[c, k]
    to = [(o, cc) for o in (0, 1, 3, 2) for cc in (0, 1)][1:]
    for i, (o, cc) in enumerate(to):
        src = tok.at[(c + cc) % 2, (k + o) % 2]
        send(src, tok_in.at[own_slot], sem(ts, i), sem(tr, own_slot), device(x, y + o, z, (c + cc) % 2))
    for o, cc in to:
        at = 2 * on_y(o) + (c + cc) % 2
        landed(tok_in.at[at], sem(tr, at))
    scores = tok_in[0]
    for i in range(1, 8):
        scores = scores + tok_in[i]

    lane = lax.broadcasted_iota(jnp.int32, (8, TOK_DP), 1)
    column = lax.broadcasted_iota(jnp.int32, (8, 128), 1)
    result = jnp.zeros((8, 128), F32)
    start = jnp.int32(0)
    for n in range(SEQ_DP):
        end = start + lengths[0, n]
        part = jnp.sum(jnp.where((lane >= start) & (lane < end), scores, 0.0), axis=1, keepdims=True)
        result = jnp.where(column == n, part, result)
        start = end

    s_red, r_red = names.take(15), names.take(16)
    at = 4 * z + x
    red[at] = result
    away = [(ox, oz) for oz in range(4) for ox in range(4)][1:]
    for i, (ox, oz) in enumerate(away):
        send(red.at[at], red.at[at], sem(s_red, i), sem(r_red, at), device(x + ox, y, z + oz, c))
    for ox, oz in away:
        there = 4 * ((z + oz) % 4) + (x + ox) % 4
        landed(red.at[there], sem(r_red, there))
    result = red[0]
    for i in range(1, 16):
        result = result + red[i]
    out[...] = result * SCALE

    for cp in sent:
        cp.wait_send()

    @pl.when(partner_zeta == 0)
    def _():
        to_units.wait_send()

    @pl.when(partner_zeta == 2)
    def _():
        to_other.wait_send()

    @pl.when((partner_zeta == 0) | (partner_zeta == 2))
    def _():
        to_query.wait_send()

    for i in range(2):
        y_beta_other(i).wait_send()
    y_beta_own().wait_send()

    @pl.when(is_own | is_other)
    def _():
        for i in range(3):
            z_beta(i, True).wait_send()
            for h in range(PARTS):
                x_alpha(i, True, h).wait_send()
        for i in range(4):
            for h in range(PARTS):
                y_alpha_own(i, x, h).wait_send()

    @pl.when(is_other)
    def _():
        for i in range(4):
            for h in range(PARTS):
                y_alpha_other(i, x, 3, h).wait_send()

    def drain_x(n, carry):
        x_beta(n, x, y, 1).wait_send()
        return carry

    lax.fori_loop(0, 12, drain_x, 0)

    @pl.when(pi != 3)
    def _():
        def drain_z(t, carry):
            for h in range(PARTS):
                z_alpha(t, x, y, h).wait_send()
            return carry

        lax.fori_loop(0, 16, drain_z, 0)

    for n in range(3):
        to_core(0, n).wait_send()
        back_to_core(0, n).wait_send()
    for m in range(5):
        to_mate(m).wait_send()

    assert names.used <= N_SEMS


def fused(train_t, query, train_g_t, query_g, pid, lengths, in_basis_t, eig_t, out_basis):
    vmem, hbm = pl.BlockSpec(memory_space=pltpu.VMEM), pl.BlockSpec(memory_space=pl.ANY)
    smem = pl.BlockSpec(memory_space=pltpu.SMEM)

    def v(shape, dtype=BF16):
        return pltpu.VMEM(shape, dtype)

    return pl.pallas_call(
        kernel,
        out_shape=jax.ShapeDtypeStruct((8, 128), F32),
        in_specs=[vmem, vmem, vmem, vmem, vmem, smem, hbm, hbm, hbm],
        out_specs=vmem,
        scratch_shapes=[
            v((2, DEPTH, LANES)),
            v((4, COLS, LANES)),
            v((COLS, DEPTH)),
            v((2, COLS, LANES), F32),
            v((COLS, LANES - TRAIN)),
            v((COLS, LANES - TRAIN)),
            v((COLS, QUART)),
            v((COLS, QUART), F32),
            v((4, ROWS, FEAT)),
            v((4, ROWS, FEAT)),
            v((4, FEAT, QUART)),
            v((ROWS, QUART), F32),
            v((ROWS, QUART)),
            v((4, CHUNK, QUART)),
            v((CHUNK, QUART)),
            v((CHUNK, QUART)),
            v((4, ROWS, QUART)),
            v((4, QUART, TOK_DP)),
            v((COLS, LANES), F32),
            v((COLS, LANES)),
            v((COLS, LANES)),
            v((2, COLS, LANES)),
            v((PAIRS, COLS, QUART)),
            v((2, 2, 8, TOK_DP), F32),
            v((8, 8, TOK_DP), F32),
            v((16, 8, 128), F32),
            pltpu.SemaphoreType.DMA((N_SEMS,)),
        ],
        compiler_params=pltpu.CompilerParams(
            collective_id=0, has_side_effects=True, vmem_limit_bytes=60 * 2**20
        ),
        cost_estimate=pl.CostEstimate(
            flops=2 * 1280 * 4736 * 592 + 8 * 896 * 592 * 1280, bytes_accessed=20 * 2**20, transcendentals=0
        ),
        name="influence",
    )(train_t, query, train_g_t, query_g, pid, lengths, in_basis_t, eig_t, out_basis)


def on_device(
    train_act,
    train_out_grad,
    query_act,
    query_out_grad,
    in_basis,
    out_basis,
    eigvals,
    pair_ids,
    seq_lengths,
):
    scores = fused(
        train_act.T,
        query_act,
        train_out_grad.T,
        query_out_grad,
        pair_ids[None, :],
        seq_lengths,
        in_basis.T,
        eigvals.T,
        out_basis,
    )
    return scores[:PAIRS, :SEQ_DP]


def solution(mesh):
    in_specs = (
        P("dp", "basis"),
        P("dp", "basis"),
        P("dp", "basis"),
        P("dp", "basis"),
        P("dp", "basis"),
        P("basis", None),
        P(None, "basis"),
        P(),
        P("dp", None),
    )
    out_specs = P(None, "dp")
    return jax.shard_map(
        on_device, mesh=mesh, in_specs=in_specs, out_specs=out_specs, check_vma=False
    )
```

```python
import functools
import math

import jax
import jax.numpy as jnp
from jax import lax
from jax.experimental import pallas as pl
from jax.experimental.pallas import tpu as pltpu
from jax.sharding import PartitionSpec as P

D = 3584
FF = 18944
PAIRS = 4
SEQ_DP = 4
TOK_DP = 256
QTOK_DP = 64
ROWS = TOK_DP + QTOK_DP
COLS = FF // 32
DEPTH = FF // 4
FEAT = D // 32
QUART = D // 4
LANES = 2 * ROWS
TRAIN = 2 * TOK_DP
CHUNK = ROWS // 4

DAMPING = 0.5
SCALE = SEQ_DP / math.sqrt(D * FF * TOK_DP * QTOK_DP)
MESH = pl.DeviceIdType.MESH
F32, BF16 = jnp.float32, jnp.bfloat16

RB = 352
PARTS = 3
RA = (COLS - RB) // PARTS
PB = 2
RP = RB // PB
OTHER = (1, 3, 2)
CHUNKS = ((TRAIN, LANES - TRAIN), (0, TOK_DP), (TOK_DP, TOK_DP))
COPIES = ((0,), (1, 2), (3, 4))


def place():
    dp, b = lax.axis_index("dp"), lax.axis_index("basis")
    return b % 4, ((b // 4) % 2) * 2 + dp // 2, b // 8, dp % 2


def device(x, y, z, c):
    x, y, z = (x + 4) % 4, (y + 4) % 4, (z + 4) % 4
    return ((y % 2) * 2 + c, z * 8 + (y // 2) * 4 + x)


class Sems:
    def __init__(self):
        self.used = 0

    def take(self, n=1):
        self.used += n
        return self.used - n


N_SEMS = 420


def kernel(
    train_t, query, train_g_t, query_g, pid, lengths, w_hbm, eig_hbm, ob_hbm, out,
    units, other, w, acc, query_t, query_in, eig, recip,
    og_tok, og_feat, ob, g_sum, g_part, g_rz, g_yb, g_ry, g_full, g_train_t,
    sum_in, chip_out, chip_in, rot, precond, tok, tok_in, red,
    sems,
):
    x, y, z, c = place()
    k = y % 2
    d = 2 * k + c
    zeta = (z - d + 4) % 4
    sign = 1 - 2 * c
    pi = (sign * zeta + 4) % 4
    is_own, is_other = zeta == 0, zeta == 2
    names = Sems()

    def sem(base, i=0):
        return sems.at[base + i]

    def slot(xs, ys):
        return ((xs + 4) % 4) * 4 + (ys + 4) % 4

    def unit(xs, ys, low, count, lanes=None):
        xs, ys = (xs + 4) % 4, (ys + 4) % 4
        rows = pl.ds(pl.multiple_of(COLS * (4 * (ys // 2) + xs) + low, 16), count)
        return units.at[ys % 2, rows] if lanes is None else units.at[ys % 2, rows, lanes]

    def beta(xs, ys, g):
        return unit(xs, ys, g * RP, RP)

    def other_beta(g):
        return other.at[x, pl.ds(g * RP, RP)]

    def got_beta(xs, ys, g):
        return sem(r_b, PB * slot(xs, ys) + g)

    def alpha(xs, ys, h):
        return unit(xs, ys, RB + h * RA, RA)

    def other_alpha(xs, h):
        return other.at[xs, pl.ds(RB + h * RA, RA)]

    def copy(src, dst, send, recv, target):
        return pltpu.make_async_remote_copy(
            src_ref=src, dst_ref=dst, send_sem=send, recv_sem=recv, device_id=target, device_id_type=MESH
        )

    partners = [device(x + o, y, z, c) for o in OTHER]
    partners += [device(x, y + o, z, c) for o in OTHER]
    partners += [device(x, y, z + o, c) for o in OTHER]
    core = device(x, y, z, 1 - c)
    partners += [core] + [device(x, y + o, z, 1 - c) for o in OTHER]
    partners += [device(x + ox, y, z + oz, c) for ox in OTHER for oz in OTHER]
    mate = device(x, y + 1 - 2 * k, z, c)

    def landed(dst, recv):
        copy(dst, dst, sem(dummy), recv, core).wait_recv()

    sent = []

    def send(src, dst, s, r, target):
        cp = copy(src, dst, s, r, target)
        cp.start()
        sent.append(cp)

    dummy = names.take()
    s_w, s_eig, s_ob, s_own = names.take(), names.take(), names.take(), names.take()
    s_step, r_step = names.take(2), names.take(2)
    r_b, r_a, r_ob, r_oa = names.take(16 * PB), names.take(16 * PARTS), names.take(PB), names.take(4 * PARTS)
    s_zb, s_yb, s_xb = names.take(3 * PB), names.take(3 * PB), names.take(12 * PB)
    s_xa, s_ya, s_ya2, s_za = (names.take(n * PARTS) for n in (3, 4, 4, 16))

    w_copy = pltpu.make_async_copy(w_hbm, w, sem(s_w))
    w_copy.start()
    quarter = pl.ds(pl.multiple_of(d * QUART, 128), QUART)
    ob_copy = pltpu.make_async_copy(ob_hbm.at[:, quarter], ob.at[x], sem(s_ob))
    ob_copy.start()
    eig_copy = pltpu.make_async_copy(eig_hbm.at[:, quarter], eig, sem(s_eig))
    eig_copy.start()

    turned = query[...].astype(F32).T.astype(BF16)
    nothing = jnp.zeros_like(turned)
    query_t[...] = jnp.concatenate(
        [jnp.where(c == 0, turned, nothing), jnp.where(c == 1, turned, nothing)], axis=1
    )
    og_tok[d, 0:TOK_DP, :] = train_g_t[...].astype(F32).T.astype(BF16)
    og_tok[d, TOK_DP:, :] = query_g[...]

    barrier = pltpu.get_barrier_semaphore()
    for p in partners:
        pl.semaphore_signal(barrier, inc=1, device_id=p, device_id_type=MESH)
    pl.semaphore_wait(barrier, len(partners))

    gs_c, gr_c = names.take(), names.take()
    send(og_tok.at[d], og_tok.at[d], sem(gs_c), sem(gr_c), core)

    mine = pl.ds(pl.multiple_of(c * TOK_DP, 128), TOK_DP)
    theirs = pl.ds(pl.multiple_of((1 - c) * TOK_DP, 128), TOK_DP)
    tail = pl.ds(TRAIN, LANES - TRAIN)
    partner_zeta = (zeta - sign + 4) % 4
    to_units = copy(train_t, unit(x, y, 0, COLS, mine), sem(s_step), sem(r_step), core)
    to_other = copy(train_t, other.at[x, :, mine], sem(s_step), sem(r_step), core)
    to_query = copy(query_t, query_in, sem(s_step, 1), sem(r_step, 1), core)

    @pl.when(partner_zeta == 0)
    def _():
        to_units.start()

    @pl.when(partner_zeta == 2)
    def _():
        to_other.start()

    @pl.when((partner_zeta == 0) | (partner_zeta == 2))
    def _():
        to_query.start()

    def z_beta(i, own, g):
        piece = beta(x, y, g) if own else other_beta(g)
        got = got_beta(x, y, g) if own else sem(r_ob, g)
        return copy(piece, piece, sem(s_zb, PB * i + g), got, device(x, y, z + OTHER[i], c))

    def got_alpha(xs, ys, h):
        return sem(r_a, PARTS * slot(xs, ys) + h)

    def x_alpha(i, own, h):
        piece = alpha(x, y, h) if own else other_alpha(x, h)
        got = got_alpha(x, y, h) if own else sem(r_oa, PARTS * x + h)
        return copy(piece, piece, sem(s_xa, PARTS * i + h), got, device(x + OTHER[i], y, z, c))

    def z_alpha(t, xs, ys, h):
        piece = alpha(xs, ys, h)
        return copy(piece, piece, sem(s_za, PARTS * t + h), got_alpha(xs, ys, h), device(x, y, z + sign, c))

    def y_alpha_own(i, xs, h):
        piece = alpha(xs, y, h)
        return copy(piece, piece, sem(s_ya, PARTS * i + h), got_alpha(xs, y, h), device(x, y + 2, z, c))

    def y_alpha_other(i, xs, step, h):
        sent_by = sem(s_ya if step == 1 else s_ya2, PARTS * i + h)
        return copy(other_alpha(xs, h), alpha(xs, y, h), sent_by, got_alpha(xs, y, h), device(x, y + step, z, c))

    def y_beta_own(g):
        piece = beta(x, y, g)
        return copy(piece, piece, sem(s_yb, 2 * PB + g), got_beta(x, y, g), device(x, y + 2, z, c))

    def y_beta_other(i, g):
        return copy(other_beta(g), beta(x, y, g), sem(s_yb, PB * i + g), got_beta(x, y, g), device(x, y + OTHER[i], z, c))

    def x_beta(n, xs, ys, step, g):
        piece = beta(xs, ys, g)
        return copy(piece, piece, sem(s_xb, PB * n + g), got_beta(xs, ys, g), device(x + step, y, z, c))

    def gather_step(dst_mine, dst_theirs, dst_tail):
        own = pltpu.make_async_copy(train_t, dst_mine, sem(s_own))
        own.start()
        own.wait()
        landed(query_in, sem(r_step, 1))
        dst_tail[...] = query_t[...] + query_in[...]
        landed(dst_theirs, sem(r_step))

    @pl.when(is_own)
    def _():
        gather_step(unit(x, y, 0, COLS, mine), unit(x, y, 0, COLS, theirs), unit(x, y, 0, COLS, tail))
        for g in range(PB):
            for i in range(3):
                z_beta(i, True, g).start()
        for i in range(3):
            for h in range(PARTS):
                x_alpha(i, True, h).start()

    @pl.when(is_other)
    def _():
        gather_step(other.at[x, :, mine], other.at[x, :, theirs], other.at[x, :, tail])
        for g in range(PB):
            for i in range(3):
                z_beta(i, False, g).start()
        for i in range(3):
            for h in range(PARTS):
                x_alpha(i, False, h).start()
        for h in range(PARTS):
            y_alpha_other(0, x, 1, h).start()
            y_alpha_other(0, x, 3, h).start()

    @pl.when(is_own)
    def _():
        for h in range(PARTS):
            y_alpha_own(0, x, h).start()

    gs_y, gr_y = names.take(2), names.take(2)
    landed(og_tok.at[2 * k + 1 - c], sem(gr_c))
    send(og_tok.at[2 * k], og_tok.at[2 * k], sem(gs_y), sem(gr_y), mate)
    send(og_tok.at[2 * k + 1], og_tok.at[2 * k + 1], sem(gs_y, 1), sem(gr_y, 1), mate)
    ob_copy.wait()
    gs_ob, gr_ob = names.take(3), names.take(4)
    for i, o in enumerate(OTHER):
        send(ob.at[x], ob.at[x], sem(gs_ob, i), sem(gr_ob, x), device(x + o, y, z, c))

    ALPHA = [(0, 0), (1, 0), (3, 0), (2, 0), (0, 2), (0, 1), (0, 3), (1, 2), (3, 2), (2, 2)]
    ALPHA += [(1, 1), (1, 3), (3, 1), (3, 3), (2, 1), (2, 3)]
    BETA = (0, 2, 1, 3)

    def on_x(o):
        return (x + o) % 4

    def on_y(o):
        return (y + o) % 4

    def alphas(first, last):
        for t in range(first, last):
            dx, dy = ALPHA[t]
            xs, ys = on_x(dx), on_y(dy)
            for h in range(PARTS):
                if (dx, dy) == (0, 0):

                    @pl.when(jnp.logical_not(is_own))
                    def _():
                        landed(alpha(xs, ys, h), got_alpha(xs, ys, h))
                else:
                    landed(alpha(xs, ys, h), got_alpha(xs, ys, h))

                @pl.when(pi != 3)
                def _():
                    z_alpha(t, xs, ys, h).start()

    def own_beta(i):
        ys = on_y(BETA[i])
        for g in range(PB):
            if i == 0:

                @pl.when(jnp.logical_not(is_own))
                def _():
                    landed(beta(x, ys, g), got_beta(x, ys, g))
            else:
                landed(beta(x, ys, g), got_beta(x, ys, g))
            x_beta(2 * i, x, ys, 1, g).start()
            x_beta(2 * i + 1, x, ys, 3, g).start()
            if i == 0:
                y_beta_own(g).start()

    def side_beta(i):
        ys = on_y(BETA[i])
        order = ((3, 1), (1, 3))[i % 2]
        for n, dx in enumerate(order):
            for g in range(PB):
                landed(beta(on_x(dx), ys, g), got_beta(on_x(dx), ys, g))
                if n == 0:
                    x_beta(8 + i, on_x(dx), ys, 4 - dx, g).start()

    def far_beta(i):
        ys = on_y(BETA[i])
        for g in range(PB):
            landed(beta(on_x(2), ys, g), got_beta(on_x(2), ys, g))

    own_beta(0)

    for g in range(PB):

        @pl.when(jnp.logical_not(is_other))
        def _():
            landed(other_beta(g), sem(r_ob, g))

        y_beta_other(0, g).start()
        y_beta_other(1, g).start()
    alphas(0, 2)

    landed(og_tok.at[2 * (1 - k)], sem(gr_y))
    landed(og_tok.at[2 * (1 - k) + 1], sem(gr_y, 1))
    gs_f, gr_f = names.take(3), names.take(4)
    for i, o in enumerate(OTHER):
        q = (x + o) % 4
        send(og_tok.at[q], og_feat.at[x], sem(gs_f, i), sem(gr_f, x), device(x + o, y, z, c))
    og_feat[x] = og_tok[x]

    own_beta(1)
    alphas(2, 4)

    for o in OTHER:
        xs = (x + o) % 4
        landed(og_feat.at[xs], sem(gr_f, xs))
        landed(ob.at[xs], sem(gr_ob, xs))

    def feature_block(i, carry):
        g_sum[...] += jnp.dot(og_feat[i], ob[i], preferred_element_type=F32)
        return carry

    g_sum[...] = jnp.zeros_like(g_sum)
    lax.fori_loop(0, 4, feature_block, 0)
    g_part[...] = g_sum[...].astype(BF16)

    def chunk(zz):
        return pl.ds(pl.multiple_of(((zz + 4) % 4) * CHUNK, 16), CHUNK)

    gs_z, gr_z = names.take(3), names.take(4)
    for i, o in enumerate(OTHER):
        send(g_part.at[chunk(z + o)], g_rz.at[z], sem(gs_z, i), sem(gr_z, z), device(x, y, z + o, c))

    side_beta(0)
    eig_copy.wait()
    recip[...] = 1.0 / (eig[...].astype(F32) + DAMPING)

    own_beta(2)
    own_beta(3)

    @pl.when(is_own)
    def _():
        for i, dx in enumerate(OTHER):
            for h in range(PARTS):
                y_alpha_own(i + 1, on_x(dx), h).start()

    @pl.when(is_other)
    def _():
        for i, dx in enumerate(OTHER):
            for h in range(PARTS):
                landed(other_alpha(on_x(dx), h), sem(r_oa, PARTS * on_x(dx) + h))
                y_alpha_other(i + 1, on_x(dx), 1, h).start()
                y_alpha_other(i + 1, on_x(dx), 3, h).start()

    alphas(4, 5)
    total = g_sum[chunk(z), :]
    for o in OTHER:
        zz = (z + o) % 4
        landed(g_rz.at[zz], sem(gr_z, zz))
        total = total + g_rz[zz].astype(F32)
    g_sum[chunk(z), :] = total
    g_yb[...] = total.astype(BF16)
    gs_h, gr_h = names.take(), names.take()
    send(g_yb, g_ry, sem(gs_h), sem(gr_h), device(x, y + 2, z, c))

    side_beta(1)
    alphas(5, 6)
    landed(g_ry, sem(gr_h))
    g_full[x, chunk(z), :] = (g_sum[chunk(z), :] + g_ry[...].astype(F32)).astype(BF16)
    gs_g, gr_g = names.take(3), names.take(4)
    for i, o in enumerate(OTHER):
        piece = g_full.at[x, chunk(z)]
        send(piece, piece, sem(gs_g, i), sem(gr_g, z), device(x, y, z + o, c))

    alphas(6, 8)
    side_beta(2)
    alphas(8, 9)
    for o in OTHER:
        zz = (z + o) % 4
        landed(g_full.at[x, chunk(zz)], sem(gr_g, zz))
    gs_x, gr_x, gs_v, gr_v = names.take(3), names.take(4), names.take(3), names.take(4)

    def rows_of(yh):
        return pl.ds(pl.multiple_of(yh * (ROWS // 2), 16), ROWS // 2)

    low, high = rows_of(y // 2), rows_of(1 - y // 2)
    for i, o in enumerate(OTHER):
        send(g_full.at[x, low], g_full.at[x, low], sem(gs_x, i), sem(gr_x, x), device(x + o, y, z, c))

    alphas(9, 10)
    far_beta(0)
    far_beta(1)
    w_copy.wait()

    def lanes(n):
        return pl.ds(*CHUNKS[n])

    def product(yl, n):
        ln = lanes(n)
        acc[yl, :, ln] = jnp.dot(w[:, 4608:], units[yl, 4608:, ln], preferred_element_type=F32)

        def body(i, carry):
            rows = pl.ds(pl.multiple_of(i * 768, 128), 768)
            acc[yl, :, ln] += jnp.dot(w[:, rows], units[yl, rows, ln], preferred_element_type=F32)
            return carry

        lax.fori_loop(0, 6, body, 0)

    s_c1, r_c1, s_m, r_m, s_c2, r_c2 = (names.take(n) for n in (3, 3, 5, 5, 3, 3))
    early, late = k, 1 - k
    sums_early = c == early
    sums_late = jnp.logical_not(sums_early)

    def along_y(m):
        return pl.ds(((m + 4) % 5) * 128, 128)

    def to_core(yl, n):
        return copy(acc.at[yl, :, lanes(n)], sum_in.at[:, lanes(n)], sem(s_c1, n), sem(r_c1, n), core)

    def to_mate(m):
        return copy(chip_out.at[:, along_y(m)], chip_in.at[:, along_y(m)], sem(s_m, m), sem(r_m, m), mate)

    def back_to_core(yl, n):
        piece = rot.at[yl, :, lanes(n)]
        return copy(piece, piece, sem(s_c2, n), sem(r_c2, n), core)

    def chip_sum(yl, n):
        ln = lanes(n)
        landed(sum_in.at[:, ln], sem(r_c1, n))
        total = acc[yl, :, ln] + sum_in[:, ln]
        acc[yl, :, ln] = total
        chip_out[:, ln] = total.astype(BF16)
        for m in COPIES[n]:
            to_mate(m).start()

    def finish(yl, n):
        ln = lanes(n)
        for m in COPIES[n]:
            landed(chip_in.at[:, along_y(m)], sem(r_m, m))
        rot[yl, :, ln] = (acc[yl, :, ln] + chip_in[:, ln].astype(F32)).astype(BF16)
        back_to_core(yl, n).start()

    for n in range(3):
        product(early, n)

        @pl.when(sums_late)
        def _():
            to_core(early, n).start()

    alphas(10, 12)
    side_beta(3)
    for i, o in enumerate(OTHER):
        q = on_x(o)
        landed(g_full.at[q, low], sem(gr_x, q))
        send(g_full.at[q, low], g_full.at[q, low], sem(gs_v, i), sem(gr_v, q), device(x, y + 2, z, c))

    @pl.when(sums_early)
    def _():
        for n in range(3):
            chip_sum(early, n)

    alphas(12, 16)
    far_beta(2)
    far_beta(3)
    def late_product(n):
        product(late, n)

        @pl.when(sums_early)
        def _():
            to_core(late, n).start()

    def late_sum(n):
        @pl.when(sums_late)
        def _():
            chip_sum(late, n)
            finish(late, n)

    late_product(0)
    late_product(1)
    late_sum(0)
    late_product(2)
    late_sum(1)
    late_sum(2)

    for o in OTHER:
        landed(g_full.at[on_x(o), high], sem(gr_v, on_x(o)))

    def transpose(q, carry):
        g_train_t[q] = g_full[q, 0:TOK_DP, :].astype(F32).T.astype(BF16)
        return carry

    lax.fori_loop(0, 4, transpose, 0)

    def finish_early(n):
        @pl.when(sums_early)
        def _():
            finish(early, n)

    def await_early(n):
        @pl.when(sums_late)
        def _():
            landed(rot.at[early, :, lanes(n)], sem(r_c2, n))

    def await_late(n):
        @pl.when(sums_early)
        def _():
            landed(rot.at[late, :, lanes(n)], sem(r_c2, n))

    finish_early(0)
    await_early(0)
    await_late(0)

    query_rot = jnp.concatenate([rot[0, :, TRAIN:], rot[1, :, TRAIN:]], axis=1).astype(F32)
    query_grad = jnp.concatenate([g_full[q, TOK_DP:, :] for q in range(4)], axis=0)
    for p in range(PAIRS):
        masked = jnp.where(pid[...] == p, query_rot, 0.0).astype(BF16)
        precond[p] = (jnp.dot(masked, query_grad, preferred_element_type=F32) * recip[...]).astype(BF16)

    def token_scores(yl, cc):
        train = rot[yl, :, lanes(1 + cc)].astype(F32)
        rows = []
        for p in range(PAIRS):
            projected = jnp.dot(precond[p], g_train_t[2 * yl + cc], preferred_element_type=F32)
            rows.append(jnp.sum(projected * train, axis=0, keepdims=True))
        rows.append(jnp.zeros((8 - PAIRS, TOK_DP), F32))
        tok[cc, yl] = jnp.concatenate(rows, axis=0)

    finish_early(1)
    await_late(1)
    token_scores(late, 0)
    finish_early(2)
    await_late(2)
    token_scores(late, 1)
    await_early(1)
    token_scores(early, 0)
    await_early(2)
    token_scores(early, 1)

    ts, tr = names.take(7), names.take(8)
    own_slot = 2 * y + c
    tok_in[own_slot] = tok[c, k]
    to = [(o, cc) for o in (0, 1, 3, 2) for cc in (0, 1)][1:]
    for i, (o, cc) in enumerate(to):
        src = tok.at[(c + cc) % 2, (k + o) % 2]
        send(src, tok_in.at[own_slot], sem(ts, i), sem(tr, own_slot), device(x, y + o, z, (c + cc) % 2))
    for o, cc in to:
        at = 2 * on_y(o) + (c + cc) % 2
        landed(tok_in.at[at], sem(tr, at))
    scores = tok_in[0]
    for i in range(1, 8):
        scores = scores + tok_in[i]

    lane = lax.broadcasted_iota(jnp.int32, (8, TOK_DP), 1)
    column = lax.broadcasted_iota(jnp.int32, (8, 128), 1)
    result = jnp.zeros((8, 128), F32)
    start = jnp.int32(0)
    for n in range(SEQ_DP):
        end = start + lengths[0, n]
        part = jnp.sum(jnp.where((lane >= start) & (lane < end), scores, 0.0), axis=1, keepdims=True)
        result = jnp.where(column == n, part, result)
        start = end

    s_red, r_red = names.take(15), names.take(16)
    at = 4 * z + x
    red[at] = result
    away = [(ox, oz) for oz in range(4) for ox in range(4)][1:]
    for i, (ox, oz) in enumerate(away):
        send(red.at[at], red.at[at], sem(s_red, i), sem(r_red, at), device(x + ox, y, z + oz, c))
    for ox, oz in away:
        there = 4 * ((z + oz) % 4) + (x + ox) % 4
        landed(red.at[there], sem(r_red, there))
    result = red[0]
    for i in range(1, 16):
        result = result + red[i]
    out[...] = result * SCALE

    for cp in sent:
        cp.wait_send()

    @pl.when(partner_zeta == 0)
    def _():
        to_units.wait_send()

    @pl.when(partner_zeta == 2)
    def _():
        to_other.wait_send()

    @pl.when((partner_zeta == 0) | (partner_zeta == 2))
    def _():
        to_query.wait_send()

    for g in range(PB):
        for i in range(2):
            y_beta_other(i, g).wait_send()
        y_beta_own(g).wait_send()

    @pl.when(is_own | is_other)
    def _():
        for i in range(3):
            for g in range(PB):
                z_beta(i, True, g).wait_send()
            for h in range(PARTS):
                x_alpha(i, True, h).wait_send()
        for i in range(4):
            for h in range(PARTS):
                y_alpha_own(i, x, h).wait_send()

    @pl.when(is_other)
    def _():
        for i in range(4):
            for h in range(PARTS):
                y_alpha_other(i, x, 3, h).wait_send()

    def drain_x(n, carry):
        for g in range(PB):
            x_beta(n, x, y, 1, g).wait_send()
        return carry

    lax.fori_loop(0, 12, drain_x, 0)

    @pl.when(pi != 3)
    def _():
        def drain_z(t, carry):
            for h in range(PARTS):
                z_alpha(t, x, y, h).wait_send()
            return carry

        lax.fori_loop(0, 16, drain_z, 0)

    for n in range(3):
        to_core(0, n).wait_send()
        back_to_core(0, n).wait_send()
    for m in range(5):
        to_mate(m).wait_send()

    assert names.used <= N_SEMS


def fused(train_t, query, train_g_t, query_g, pid, lengths, in_basis_t, eig_t, out_basis):
    vmem, hbm = pl.BlockSpec(memory_space=pltpu.VMEM), pl.BlockSpec(memory_space=pl.ANY)
    smem = pl.BlockSpec(memory_space=pltpu.SMEM)

    def v(shape, dtype=BF16):
        return pltpu.VMEM(shape, dtype)

    return pl.pallas_call(
        kernel,
        out_shape=jax.ShapeDtypeStruct((8, 128), F32),
        in_specs=[vmem, vmem, vmem, vmem, vmem, smem, hbm, hbm, hbm],
        out_specs=vmem,
        scratch_shapes=[
            v((2, DEPTH, LANES)),
            v((4, COLS, LANES)),
            v((COLS, DEPTH)),
            v((2, COLS, LANES), F32),
            v((COLS, LANES - TRAIN)),
            v((COLS, LANES - TRAIN)),
            v((COLS, QUART)),
            v((COLS, QUART), F32),
            v((4, ROWS, FEAT)),
            v((4, ROWS, FEAT)),
            v((4, FEAT, QUART)),
            v((ROWS, QUART), F32),
            v((ROWS, QUART)),
            v((4, CHUNK, QUART)),
            v((CHUNK, QUART)),
            v((CHUNK, QUART)),
            v((4, ROWS, QUART)),
            v((4, QUART, TOK_DP)),
            v((COLS, LANES), F32),
            v((COLS, LANES)),
            v((COLS, LANES)),
            v((2, COLS, LANES)),
            v((PAIRS, COLS, QUART)),
            v((2, 2, 8, TOK_DP), F32),
            v((8, 8, TOK_DP), F32),
            v((16, 8, 128), F32),
            pltpu.SemaphoreType.DMA((N_SEMS,)),
        ],
        compiler_params=pltpu.CompilerParams(
            collective_id=0, has_side_effects=True, vmem_limit_bytes=60 * 2**20
        ),
        cost_estimate=pl.CostEstimate(
            flops=2 * 1280 * 4736 * 592 + 8 * 896 * 592 * 1280, bytes_accessed=20 * 2**20, transcendentals=0
        ),
        name="influence",
    )(train_t, query, train_g_t, query_g, pid, lengths, in_basis_t, eig_t, out_basis)


def on_device(
    train_act,
    train_out_grad,
    query_act,
    query_out_grad,
    in_basis,
    out_basis,
    eigvals,
    pair_ids,
    seq_lengths,
):
    scores = fused(
        train_act.T,
        query_act,
        train_out_grad.T,
        query_out_grad,
        pair_ids[None, :],
        seq_lengths,
        in_basis.T,
        eigvals.T,
        out_basis,
    )
    return scores[:PAIRS, :SEQ_DP]


def solution(mesh):
    in_specs = (
        P("dp", "basis"),
        P("dp", "basis"),
        P("dp", "basis"),
        P("dp", "basis"),
        P("dp", "basis"),
        P("basis", None),
        P(None, "basis"),
        P(),
        P("dp", None),
    )
    out_specs = P(None, "dp")
    return jax.shard_map(
        on_device, mesh=mesh, in_specs=in_specs, out_specs=out_specs, check_vma=False
    )
```

```python
import functools
import math

import jax
import jax.numpy as jnp
from jax import lax
from jax.experimental import pallas as pl
from jax.experimental.pallas import tpu as pltpu
from jax.sharding import PartitionSpec as P

D = 3584
FF = 18944
PAIRS = 4
SEQ_DP = 4
TOK_DP = 256
QTOK_DP = 64
ROWS = TOK_DP + QTOK_DP
COLS = FF // 32
DEPTH = FF // 4
FEAT = D // 32
QUART = D // 4
LANES = 2 * ROWS
TRAIN = 2 * TOK_DP
CHUNK = ROWS // 4

DAMPING = 0.5
SCALE = SEQ_DP / math.sqrt(D * FF * TOK_DP * QTOK_DP)
MESH = pl.DeviceIdType.MESH
F32, BF16 = jnp.float32, jnp.bfloat16

RB = 352
PARTS = 3
RA = (COLS - RB) // PARTS
PB = 2
RP = RB // PB
OTHER = (1, 3, 2)
CHUNKS = ((TRAIN, LANES - TRAIN), (0, TOK_DP), (TOK_DP, TOK_DP))
COPIES = ((0,), (1, 2), (3, 4))


def place():
    dp, b = lax.axis_index("dp"), lax.axis_index("basis")
    return b % 4, ((b // 4) % 2) * 2 + dp // 2, b // 8, dp % 2


def device(x, y, z, c):
    x, y, z = (x + 4) % 4, (y + 4) % 4, (z + 4) % 4
    return ((y % 2) * 2 + c, z * 8 + (y // 2) * 4 + x)


class Sems:
    def __init__(self):
        self.used = 0

    def take(self, n=1):
        self.used += n
        return self.used - n


N_SEMS = 420


def kernel(
    train_t, query, train_g_t, query_g, pid, lengths, w_hbm, eig_hbm, ob_hbm, out,
    units, other, w, acc, query_t, query_in, eig, recip,
    og_tok, og_feat, ob, g_sum, g_part, g_rz, g_yb, g_ry, g_full, g_train_t,
    sum_in, chip_out, chip_in, rot, precond, tok, tok_in, red,
    sems,
):
    x, y, z, c = place()
    k = y % 2
    d = 2 * k + c
    zeta = (z - d + 4) % 4
    sign = 1 - 2 * c
    pi = (sign * zeta + 4) % 4
    is_own, is_other = zeta == 0, zeta == 2
    names = Sems()

    def sem(base, i=0):
        return sems.at[base + i]

    def slot(xs, ys):
        return ((xs + 4) % 4) * 4 + (ys + 4) % 4

    def unit(xs, ys, low, count, lanes=None):
        xs, ys = (xs + 4) % 4, (ys + 4) % 4
        rows = pl.ds(pl.multiple_of(COLS * (4 * (ys // 2) + xs) + low, 16), count)
        return units.at[ys % 2, rows] if lanes is None else units.at[ys % 2, rows, lanes]

    def beta(xs, ys, g):
        return unit(xs, ys, g * RP, RP)

    def other_beta(g):
        return other.at[x, pl.ds(g * RP, RP)]

    def got_beta(xs, ys, g):
        return sem(r_b, PB * slot(xs, ys) + g)

    def alpha(xs, ys, h):
        return unit(xs, ys, RB + h * RA, RA)

    def other_alpha(xs, h):
        return other.at[xs, pl.ds(RB + h * RA, RA)]

    def copy(src, dst, send, recv, target):
        return pltpu.make_async_remote_copy(
            src_ref=src, dst_ref=dst, send_sem=send, recv_sem=recv, device_id=target, device_id_type=MESH
        )

    partners = [device(x + o, y, z, c) for o in OTHER]
    partners += [device(x, y + o, z, c) for o in OTHER]
    partners += [device(x, y, z + o, c) for o in OTHER]
    core = device(x, y, z, 1 - c)
    partners += [core] + [device(x, y + o, z, 1 - c) for o in OTHER]
    partners += [device(x + ox, y, z + oz, c) for ox in OTHER for oz in OTHER]
    mate = device(x, y + 1 - 2 * k, z, c)

    def landed(dst, recv):
        copy(dst, dst, sem(dummy), recv, core).wait_recv()

    sent = []

    def send(src, dst, s, r, target):
        cp = copy(src, dst, s, r, target)
        cp.start()
        sent.append(cp)

    dummy = names.take()
    s_w, s_eig, s_ob, s_own = names.take(), names.take(), names.take(), names.take()
    s_step, r_step = names.take(2), names.take(2)
    r_b, r_a, r_ob, r_oa = names.take(16 * PB), names.take(16 * PARTS), names.take(PB), names.take(4 * PARTS)
    s_zb, s_yb, s_xb = names.take(3 * PB), names.take(3 * PB), names.take(12 * PB)
    s_xa, s_ya, s_ya2, s_za = (names.take(n * PARTS) for n in (3, 4, 4, 16))

    w_copy = pltpu.make_async_copy(w_hbm, w, sem(s_w))
    w_copy.start()
    quarter = pl.ds(pl.multiple_of(d * QUART, 128), QUART)
    ob_copy = pltpu.make_async_copy(ob_hbm.at[:, quarter], ob.at[x], sem(s_ob))
    ob_copy.start()
    eig_copy = pltpu.make_async_copy(eig_hbm.at[:, quarter], eig, sem(s_eig))
    eig_copy.start()

    turned = query[...].astype(F32).T.astype(BF16)
    nothing = jnp.zeros_like(turned)
    query_t[...] = jnp.concatenate(
        [jnp.where(c == 0, turned, nothing), jnp.where(c == 1, turned, nothing)], axis=1
    )
    og_tok[d, 0:TOK_DP, :] = train_g_t[...].astype(F32).T.astype(BF16)
    og_tok[d, TOK_DP:, :] = query_g[...]

    barrier = pltpu.get_barrier_semaphore()
    for p in partners:
        pl.semaphore_signal(barrier, inc=1, device_id=p, device_id_type=MESH)
    pl.semaphore_wait(barrier, len(partners))

    gs_c, gr_c = names.take(), names.take()
    send(og_tok.at[d], og_tok.at[d], sem(gs_c), sem(gr_c), core)

    ob_copy.wait()
    gs_ob, gr_ob = names.take(3), names.take(4)
    for i, o in enumerate(OTHER):
        send(ob.at[x], ob.at[x], sem(gs_ob, i), sem(gr_ob, x), device(x + o, y, z, c))

    mine = pl.ds(pl.multiple_of(c * TOK_DP, 128), TOK_DP)
    theirs = pl.ds(pl.multiple_of((1 - c) * TOK_DP, 128), TOK_DP)
    tail = pl.ds(TRAIN, LANES - TRAIN)
    partner_zeta = (zeta - sign + 4) % 4
    to_units = copy(train_t, unit(x, y, 0, COLS, mine), sem(s_step), sem(r_step), core)
    to_other = copy(train_t, other.at[x, :, mine], sem(s_step), sem(r_step), core)
    to_query = copy(query_t, query_in, sem(s_step, 1), sem(r_step, 1), core)

    @pl.when(partner_zeta == 0)
    def _():
        to_units.start()

    @pl.when(partner_zeta == 2)
    def _():
        to_other.start()

    @pl.when((partner_zeta == 0) | (partner_zeta == 2))
    def _():
        to_query.start()

    def z_beta(i, own, g):
        piece = beta(x, y, g) if own else other_beta(g)
        got = got_beta(x, y, g) if own else sem(r_ob, g)
        return copy(piece, piece, sem(s_zb, PB * i + g), got, device(x, y, z + OTHER[i], c))

    def got_alpha(xs, ys, h):
        return sem(r_a, PARTS * slot(xs, ys) + h)

    def x_alpha(i, own, h):
        piece = alpha(x, y, h) if own else other_alpha(x, h)
        got = got_alpha(x, y, h) if own else sem(r_oa, PARTS * x + h)
        return copy(piece, piece, sem(s_xa, PARTS * i + h), got, device(x + OTHER[i], y, z, c))

    def z_alpha(t, xs, ys, h):
        piece = alpha(xs, ys, h)
        return copy(piece, piece, sem(s_za, PARTS * t + h), got_alpha(xs, ys, h), device(x, y, z + sign, c))

    def y_alpha_own(i, xs, h):
        piece = alpha(xs, y, h)
        return copy(piece, piece, sem(s_ya, PARTS * i + h), got_alpha(xs, y, h), device(x, y + 2, z, c))

    def y_alpha_other(i, xs, step, h):
        sent_by = sem(s_ya if step == 1 else s_ya2, PARTS * i + h)
        return copy(other_alpha(xs, h), alpha(xs, y, h), sent_by, got_alpha(xs, y, h), device(x, y + step, z, c))

    def y_beta_own(g):
        piece = beta(x, y, g)
        return copy(piece, piece, sem(s_yb, 2 * PB + g), got_beta(x, y, g), device(x, y + 2, z, c))

    def y_beta_other(i, g):
        return copy(other_beta(g), beta(x, y, g), sem(s_yb, PB * i + g), got_beta(x, y, g), device(x, y + OTHER[i], z, c))

    def x_beta(n, xs, ys, step, g):
        piece = beta(xs, ys, g)
        return copy(piece, piece, sem(s_xb, PB * n + g), got_beta(xs, ys, g), device(x + step, y, z, c))

    def gather_step(dst_mine, dst_theirs, dst_tail):
        own = pltpu.make_async_copy(train_t, dst_mine, sem(s_own))
        own.start()
        own.wait()
        landed(query_in, sem(r_step, 1))
        dst_tail[...] = query_t[...] + query_in[...]
        landed(dst_theirs, sem(r_step))

    @pl.when(is_own)
    def _():
        gather_step(unit(x, y, 0, COLS, mine), unit(x, y, 0, COLS, theirs), unit(x, y, 0, COLS, tail))
        for g in range(PB):
            for i in range(3):
                z_beta(i, True, g).start()
        for i in range(3):
            for h in range(PARTS):
                x_alpha(i, True, h).start()

    @pl.when(is_other)
    def _():
        gather_step(other.at[x, :, mine], other.at[x, :, theirs], other.at[x, :, tail])
        for g in range(PB):
            for i in range(3):
                z_beta(i, False, g).start()
        for i in range(3):
            for h in range(PARTS):
                x_alpha(i, False, h).start()
        for h in range(PARTS):
            y_alpha_other(0, x, 1, h).start()
            y_alpha_other(0, x, 3, h).start()

    @pl.when(is_own)
    def _():
        for h in range(PARTS):
            y_alpha_own(0, x, h).start()

    gs_y, gr_y = names.take(2), names.take(2)
    landed(og_tok.at[2 * k + 1 - c], sem(gr_c))
    send(og_tok.at[2 * k], og_tok.at[2 * k], sem(gs_y), sem(gr_y), mate)
    send(og_tok.at[2 * k + 1], og_tok.at[2 * k + 1], sem(gs_y, 1), sem(gr_y, 1), mate)
    ALPHA = [(0, 0), (1, 0), (3, 0), (2, 0), (0, 2), (0, 1), (0, 3), (1, 2), (3, 2), (2, 2)]
    ALPHA += [(1, 1), (1, 3), (3, 1), (3, 3), (2, 1), (2, 3)]
    BETA = (0, 2, 1, 3)

    def on_x(o):
        return (x + o) % 4

    def on_y(o):
        return (y + o) % 4

    def alphas(first, last):
        for t in range(first, last):
            dx, dy = ALPHA[t]
            xs, ys = on_x(dx), on_y(dy)
            for h in range(PARTS):
                if (dx, dy) == (0, 0):

                    @pl.when(jnp.logical_not(is_own))
                    def _():
                        landed(alpha(xs, ys, h), got_alpha(xs, ys, h))
                else:
                    landed(alpha(xs, ys, h), got_alpha(xs, ys, h))

                @pl.when(pi != 3)
                def _():
                    z_alpha(t, xs, ys, h).start()

    def own_beta(i):
        ys = on_y(BETA[i])
        for g in range(PB):
            if i == 0:

                @pl.when(jnp.logical_not(is_own))
                def _():
                    landed(beta(x, ys, g), got_beta(x, ys, g))
            else:
                landed(beta(x, ys, g), got_beta(x, ys, g))
            x_beta(2 * i, x, ys, 1, g).start()
            x_beta(2 * i + 1, x, ys, 3, g).start()
            if i == 0:
                y_beta_own(g).start()

    def side_beta(i):
        ys = on_y(BETA[i])
        order = ((3, 1), (1, 3))[i % 2]
        for n, dx in enumerate(order):
            for g in range(PB):
                landed(beta(on_x(dx), ys, g), got_beta(on_x(dx), ys, g))
                if n == 0:
                    x_beta(8 + i, on_x(dx), ys, 4 - dx, g).start()

    def far_beta(i):
        ys = on_y(BETA[i])
        for g in range(PB):
            landed(beta(on_x(2), ys, g), got_beta(on_x(2), ys, g))

    own_beta(0)

    for g in range(PB):

        @pl.when(jnp.logical_not(is_other))
        def _():
            landed(other_beta(g), sem(r_ob, g))

        y_beta_other(0, g).start()
        y_beta_other(1, g).start()
    alphas(0, 2)

    landed(og_tok.at[2 * (1 - k)], sem(gr_y))
    landed(og_tok.at[2 * (1 - k) + 1], sem(gr_y, 1))
    gs_f, gr_f = names.take(3), names.take(4)
    for i, o in enumerate(OTHER):
        q = (x + o) % 4
        send(og_tok.at[q], og_feat.at[x], sem(gs_f, i), sem(gr_f, x), device(x + o, y, z, c))
    og_feat[x] = og_tok[x]

    own_beta(1)
    alphas(2, 4)

    @pl.when(is_own)
    def _():
        for i, dx in enumerate(OTHER):
            for h in range(PARTS):
                y_alpha_own(i + 1, on_x(dx), h).start()

    @pl.when(is_other)
    def _():
        for i, dx in enumerate(OTHER):
            for h in range(PARTS):
                landed(other_alpha(on_x(dx), h), sem(r_oa, PARTS * on_x(dx) + h))
                y_alpha_other(i + 1, on_x(dx), 1, h).start()
                y_alpha_other(i + 1, on_x(dx), 3, h).start()


    for o in OTHER:
        xs = (x + o) % 4
        landed(og_feat.at[xs], sem(gr_f, xs))
        landed(ob.at[xs], sem(gr_ob, xs))

    def feature_block(i, carry):
        g_sum[...] += jnp.dot(og_feat[i], ob[i], preferred_element_type=F32)
        return carry

    g_sum[...] = jnp.zeros_like(g_sum)
    lax.fori_loop(0, 4, feature_block, 0)
    g_part[...] = g_sum[...].astype(BF16)

    def chunk(zz):
        return pl.ds(pl.multiple_of(((zz + 4) % 4) * CHUNK, 16), CHUNK)

    gs_z, gr_z = names.take(3), names.take(4)
    for i, o in enumerate(OTHER):
        send(g_part.at[chunk(z + o)], g_rz.at[z], sem(gs_z, i), sem(gr_z, z), device(x, y, z + o, c))

    side_beta(0)
    eig_copy.wait()
    recip[...] = 1.0 / (eig[...].astype(F32) + DAMPING)

    own_beta(2)
    own_beta(3)

    alphas(4, 5)
    total = g_sum[chunk(z), :]
    for o in OTHER:
        zz = (z + o) % 4
        landed(g_rz.at[zz], sem(gr_z, zz))
        total = total + g_rz[zz].astype(F32)
    g_sum[chunk(z), :] = total
    g_yb[...] = total.astype(BF16)
    gs_h, gr_h = names.take(), names.take()
    send(g_yb, g_ry, sem(gs_h), sem(gr_h), device(x, y + 2, z, c))

    side_beta(1)
    alphas(5, 6)
    landed(g_ry, sem(gr_h))
    g_full[x, chunk(z), :] = (g_sum[chunk(z), :] + g_ry[...].astype(F32)).astype(BF16)
    gs_g, gr_g = names.take(3), names.take(4)
    for i, o in enumerate(OTHER):
        piece = g_full.at[x, chunk(z)]
        send(piece, piece, sem(gs_g, i), sem(gr_g, z), device(x, y, z + o, c))

    alphas(6, 8)
    side_beta(2)
    alphas(8, 9)
    for o in OTHER:
        zz = (z + o) % 4
        landed(g_full.at[x, chunk(zz)], sem(gr_g, zz))
    gs_x, gr_x, gs_v, gr_v = names.take(3), names.take(4), names.take(3), names.take(4)

    def rows_of(yh):
        return pl.ds(pl.multiple_of(yh * (ROWS // 2), 16), ROWS // 2)

    low, high = rows_of(y // 2), rows_of(1 - y // 2)
    for i, o in enumerate(OTHER):
        send(g_full.at[x, low], g_full.at[x, low], sem(gs_x, i), sem(gr_x, x), device(x + o, y, z, c))

    alphas(9, 10)
    far_beta(0)
    far_beta(1)
    w_copy.wait()

    def lanes(n):
        return pl.ds(*CHUNKS[n])

    def product(yl, n):
        ln = lanes(n)
        acc[yl, :, ln] = jnp.dot(w[:, 4608:], units[yl, 4608:, ln], preferred_element_type=F32)

        def body(i, carry):
            rows = pl.ds(pl.multiple_of(i * 768, 128), 768)
            acc[yl, :, ln] += jnp.dot(w[:, rows], units[yl, rows, ln], preferred_element_type=F32)
            return carry

        lax.fori_loop(0, 6, body, 0)

    s_c1, r_c1, s_m, r_m, s_c2, r_c2 = (names.take(n) for n in (3, 3, 5, 5, 3, 3))
    early, late = k, 1 - k
    sums_early = c == early
    sums_late = jnp.logical_not(sums_early)

    def along_y(m):
        return pl.ds(((m + 4) % 5) * 128, 128)

    def to_core(yl, n):
        return copy(acc.at[yl, :, lanes(n)], sum_in.at[:, lanes(n)], sem(s_c1, n), sem(r_c1, n), core)

    def to_mate(m):
        return copy(chip_out.at[:, along_y(m)], chip_in.at[:, along_y(m)], sem(s_m, m), sem(r_m, m), mate)

    def back_to_core(yl, n):
        piece = rot.at[yl, :, lanes(n)]
        return copy(piece, piece, sem(s_c2, n), sem(r_c2, n), core)

    def chip_sum(yl, n):
        ln = lanes(n)
        landed(sum_in.at[:, ln], sem(r_c1, n))
        total = acc[yl, :, ln] + sum_in[:, ln]
        acc[yl, :, ln] = total
        chip_out[:, ln] = total.astype(BF16)
        for m in COPIES[n]:
            to_mate(m).start()

    def finish(yl, n):
        ln = lanes(n)
        for m in COPIES[n]:
            landed(chip_in.at[:, along_y(m)], sem(r_m, m))
        rot[yl, :, ln] = (acc[yl, :, ln] + chip_in[:, ln].astype(F32)).astype(BF16)
        back_to_core(yl, n).start()

    for n in range(3):
        product(early, n)

        @pl.when(sums_late)
        def _():
            to_core(early, n).start()

    alphas(10, 12)
    side_beta(3)
    for i, o in enumerate(OTHER):
        q = on_x(o)
        landed(g_full.at[q, low], sem(gr_x, q))
        send(g_full.at[q, low], g_full.at[q, low], sem(gs_v, i), sem(gr_v, q), device(x, y + 2, z, c))

    @pl.when(sums_early)
    def _():
        for n in range(3):
            chip_sum(early, n)

    alphas(12, 16)
    far_beta(2)
    far_beta(3)
    def late_product(n):
        product(late, n)

        @pl.when(sums_early)
        def _():
            to_core(late, n).start()

    def late_sum(n):
        @pl.when(sums_late)
        def _():
            chip_sum(late, n)
            finish(late, n)

    late_product(0)
    late_product(1)
    late_sum(0)
    late_product(2)
    late_sum(1)
    late_sum(2)

    for o in OTHER:
        landed(g_full.at[on_x(o), high], sem(gr_v, on_x(o)))

    def transpose(q, carry):
        g_train_t[q] = g_full[q, 0:TOK_DP, :].astype(F32).T.astype(BF16)
        return carry

    lax.fori_loop(0, 4, transpose, 0)

    def finish_early(n):
        @pl.when(sums_early)
        def _():
            finish(early, n)

    def await_early(n):
        @pl.when(sums_late)
        def _():
            landed(rot.at[early, :, lanes(n)], sem(r_c2, n))

    def await_late(n):
        @pl.when(sums_early)
        def _():
            landed(rot.at[late, :, lanes(n)], sem(r_c2, n))

    finish_early(0)
    await_early(0)
    await_late(0)

    query_rot = jnp.concatenate([rot[0, :, TRAIN:], rot[1, :, TRAIN:]], axis=1).astype(F32)
    query_grad = jnp.concatenate([g_full[q, TOK_DP:, :] for q in range(4)], axis=0)
    for p in range(PAIRS):
        masked = jnp.where(pid[...] == p, query_rot, 0.0).astype(BF16)
        precond[p] = (jnp.dot(masked, query_grad, preferred_element_type=F32) * recip[...]).astype(BF16)

    def token_scores(yl, cc):
        train = rot[yl, :, lanes(1 + cc)].astype(F32)
        rows = []
        for p in range(PAIRS):
            projected = jnp.dot(precond[p], g_train_t[2 * yl + cc], preferred_element_type=F32)
            rows.append(jnp.sum(projected * train, axis=0, keepdims=True))
        rows.append(jnp.zeros((8 - PAIRS, TOK_DP), F32))
        tok[cc, yl] = jnp.concatenate(rows, axis=0)

    finish_early(1)
    await_late(1)
    token_scores(late, 0)
    finish_early(2)
    await_late(2)
    token_scores(late, 1)
    await_early(1)
    token_scores(early, 0)
    await_early(2)
    token_scores(early, 1)

    ts, tr = names.take(7), names.take(8)
    own_slot = 2 * y + c
    tok_in[own_slot] = tok[c, k]
    to = [(o, cc) for o in (0, 1, 3, 2) for cc in (0, 1)][1:]
    for i, (o, cc) in enumerate(to):
        src = tok.at[(c + cc) % 2, (k + o) % 2]
        send(src, tok_in.at[own_slot], sem(ts, i), sem(tr, own_slot), device(x, y + o, z, (c + cc) % 2))
    for o, cc in to:
        at = 2 * on_y(o) + (c + cc) % 2
        landed(tok_in.at[at], sem(tr, at))
    scores = tok_in[0]
    for i in range(1, 8):
        scores = scores + tok_in[i]

    lane = lax.broadcasted_iota(jnp.int32, (8, TOK_DP), 1)
    column = lax.broadcasted_iota(jnp.int32, (8, 128), 1)
    result = jnp.zeros((8, 128), F32)
    start = jnp.int32(0)
    for n in range(SEQ_DP):
        end = start + lengths[0, n]
        part = jnp.sum(jnp.where((lane >= start) & (lane < end), scores, 0.0), axis=1, keepdims=True)
        result = jnp.where(column == n, part, result)
        start = end

    s_red, r_red = names.take(15), names.take(16)
    at = 4 * z + x
    red[at] = result
    away = [(ox, oz) for oz in range(4) for ox in range(4)][1:]
    for i, (ox, oz) in enumerate(away):
        send(red.at[at], red.at[at], sem(s_red, i), sem(r_red, at), device(x + ox, y, z + oz, c))
    for ox, oz in away:
        there = 4 * ((z + oz) % 4) + (x + ox) % 4
        landed(red.at[there], sem(r_red, there))
    result = red[0]
    for i in range(1, 16):
        result = result + red[i]
    out[...] = result * SCALE

    for cp in sent:
        cp.wait_send()

    @pl.when(partner_zeta == 0)
    def _():
        to_units.wait_send()

    @pl.when(partner_zeta == 2)
    def _():
        to_other.wait_send()

    @pl.when((partner_zeta == 0) | (partner_zeta == 2))
    def _():
        to_query.wait_send()

    for g in range(PB):
        for i in range(2):
            y_beta_other(i, g).wait_send()
        y_beta_own(g).wait_send()

    @pl.when(is_own | is_other)
    def _():
        for i in range(3):
            for g in range(PB):
                z_beta(i, True, g).wait_send()
            for h in range(PARTS):
                x_alpha(i, True, h).wait_send()
        for i in range(4):
            for h in range(PARTS):
                y_alpha_own(i, x, h).wait_send()

    @pl.when(is_other)
    def _():
        for i in range(4):
            for h in range(PARTS):
                y_alpha_other(i, x, 3, h).wait_send()

    def drain_x(n, carry):
        for g in range(PB):
            x_beta(n, x, y, 1, g).wait_send()
        return carry

    lax.fori_loop(0, 12, drain_x, 0)

    @pl.when(pi != 3)
    def _():
        def drain_z(t, carry):
            for h in range(PARTS):
                z_alpha(t, x, y, h).wait_send()
            return carry

        lax.fori_loop(0, 16, drain_z, 0)

    for n in range(3):
        to_core(0, n).wait_send()
        back_to_core(0, n).wait_send()
    for m in range(5):
        to_mate(m).wait_send()

    assert names.used <= N_SEMS


def fused(train_t, query, train_g_t, query_g, pid, lengths, in_basis_t, eig_t, out_basis):
    vmem, hbm = pl.BlockSpec(memory_space=pltpu.VMEM), pl.BlockSpec(memory_space=pl.ANY)
    smem = pl.BlockSpec(memory_space=pltpu.SMEM)

    def v(shape, dtype=BF16):
        return pltpu.VMEM(shape, dtype)

    return pl.pallas_call(
        kernel,
        out_shape=jax.ShapeDtypeStruct((8, 128), F32),
        in_specs=[vmem, vmem, vmem, vmem, vmem, smem, hbm, hbm, hbm],
        out_specs=vmem,
        scratch_shapes=[
            v((2, DEPTH, LANES)),
            v((4, COLS, LANES)),
            v((COLS, DEPTH)),
            v((2, COLS, LANES), F32),
            v((COLS, LANES - TRAIN)),
            v((COLS, LANES - TRAIN)),
            v((COLS, QUART)),
            v((COLS, QUART), F32),
            v((4, ROWS, FEAT)),
            v((4, ROWS, FEAT)),
            v((4, FEAT, QUART)),
            v((ROWS, QUART), F32),
            v((ROWS, QUART)),
            v((4, CHUNK, QUART)),
            v((CHUNK, QUART)),
            v((CHUNK, QUART)),
            v((4, ROWS, QUART)),
            v((4, QUART, TOK_DP)),
            v((COLS, LANES), F32),
            v((COLS, LANES)),
            v((COLS, LANES)),
            v((2, COLS, LANES)),
            v((PAIRS, COLS, QUART)),
            v((2, 2, 8, TOK_DP), F32),
            v((8, 8, TOK_DP), F32),
            v((16, 8, 128), F32),
            pltpu.SemaphoreType.DMA((N_SEMS,)),
        ],
        compiler_params=pltpu.CompilerParams(
            collective_id=0, has_side_effects=True, vmem_limit_bytes=60 * 2**20
        ),
        cost_estimate=pl.CostEstimate(
            flops=2 * 1280 * 4736 * 592 + 8 * 896 * 592 * 1280, bytes_accessed=20 * 2**20, transcendentals=0
        ),
        name="influence",
    )(train_t, query, train_g_t, query_g, pid, lengths, in_basis_t, eig_t, out_basis)


def on_device(
    train_act,
    train_out_grad,
    query_act,
    query_out_grad,
    in_basis,
    out_basis,
    eigvals,
    pair_ids,
    seq_lengths,
):
    scores = fused(
        train_act.T,
        query_act,
        train_out_grad.T,
        query_out_grad,
        pair_ids[None, :],
        seq_lengths,
        in_basis.T,
        eigvals.T,
        out_basis,
    )
    return scores[:PAIRS, :SEQ_DP]


def solution(mesh):
    in_specs = (
        P("dp", "basis"),
        P("dp", "basis"),
        P("dp", "basis"),
        P("dp", "basis"),
        P("dp", "basis"),
        P("basis", None),
        P(None, "basis"),
        P(),
        P("dp", None),
    )
    out_specs = P(None, "dp")
    return jax.shard_map(
        on_device, mesh=mesh, in_specs=in_specs, out_specs=out_specs, check_vma=False
    )
```
